32 devices in a mesh: freq: 8 (over z, x), depth: 4 (over y, core).
Axes of the slice: x: 2, y: 2, z: 4, core: 2. Of those that a mesh axis runs over, the one named last changes fastest.
Arguments:
- slowness: float32 [4, 24576], P('depth', 'freq'), may hold values from 0.25 to 1
- freq_index: int32 [16], P('freq'), may hold values from 0 to 15, each once
- taps: float32 [16, 2, 11], replicated, may hold values from -1 to 1, as said below
- source_top: float32 [16, 4, 2, 24, 1024], P('freq', 'depth'), may hold values from -6 to 6
- adjoint_source: float32 [16, 4, 2, 24, 1024], P('freq', 'depth'), may hold values from -6 to 6
Outputs:
- gradient: float32 [4, 24576], P('depth', 'freq')
The draws below stay inside these ranges and needn't reach their ends.
Inputs may be any that keep to these rules, and one draw needn't show every extreme that they name: `freq_index`: each of 0 to 15 appears once. In each frequency the absolute values of the complex taps sum to at most 1.
All inputs are finite; a program needn't handle non-finite values.
Results may differ from the reference program's by a relative error of at most 0.0003.
Values sent between devices are 32-bit elements; how exact they have to be, the bound alone decides.
A program may use at most 64 MiB of HBM per device.

```python
import math
import jax
import jax.numpy as jnp
from jax import lax

NX = 1024
YW = 24
TAPS = 11
FREQS = 16
NSEC = 4
NZ = 4


def draw_taps(key, part):
    keys = jax.random.split(key, 3)
    center = jax.random.uniform(keys[0], (FREQS, 1), jnp.float32, 0.7, 0.99)
    angle = jax.random.uniform(keys[1], (FREQS, TAPS), jnp.float32, -math.pi, math.pi)
    side = jax.random.uniform(keys[2], (FREQS, TAPS), jnp.float32, 0.5, 1.0) * (1.0 - center) / (TAPS - 1)
    middle = jnp.arange(TAPS) == TAPS // 2
    magnitude = jnp.where(middle[None, :], center, side)
    return jnp.stack([magnitude * jnp.cos(angle), magnitude * jnp.sin(angle)], axis=1).astype(jnp.float32)


def levels(stream_key, shape, cuts, smallest, largest):
    def one(dim, blocks):
        heights = jax.random.uniform(jax.random.fold_in(jax.random.fold_in(stream_key, 6), dim), (blocks,), jnp.float32, smallest / len(cuts), largest / len(cuts))
        return jnp.repeat(jnp.exp(heights), shape[dim] // blocks).reshape((-1,) + (1,) * (len(shape) - dim - 1))

    gain = one(*cuts[0])
    for cut in cuts[1:]:
        gain = gain * one(*cut)
    return gain


def gaussian(rng, dims, width, bound, pieces=(), kind=jnp.bfloat16):
    drawn = width * jax.random.normal(rng, dims, jnp.float32)
    if pieces:
        drawn = drawn * levels(rng, dims, pieces, -0.22, 0.18)
    return jnp.clip(drawn, -bound, bound).astype(kind)


def setup_inputs(seed: int = 0) -> dict:
    streams_of = jax.random.split(jax.random.key(seed), 6)
    slowness = jnp.clip(jnp.exp(math.log(1.0) - 1.3862944 * jax.random.uniform(streams_of[0], (NZ, YW * NX), jnp.float32) ** levels(streams_of[0], (NZ, YW * NX), ((0, 4), (1, 8)), -0.2, 0.2)), 0.25, 1.0)
    freq_index = jax.random.permutation(streams_of[1], FREQS).astype(jnp.int32)
    taps = draw_taps(jax.random.fold_in(streams_of[5], 71), 0)
    source_top = gaussian(streams_of[3], (FREQS, NSEC, 2, YW, NX), 1.0, 6.0, ((0, 8), (1, 4)), jnp.float32)
    adjoint_source = gaussian(streams_of[4], (FREQS, NZ, 2, YW, NX), 1.0, 6.0, ((0, 8), (1, 4)), jnp.float32)
    return dict(slowness=slowness, freq_index=freq_index, taps=taps, source_top=source_top, adjoint_source=adjoint_source)


def convolve(field_re, field_im, tap_re, tap_im, along, adjoint):
    along = field_re.ndim + along
    reach = tap_re.shape[-1] // 2
    extent = field_re.shape[along]
    widths = [(0, 0)] * field_re.ndim
    widths[along] = (reach, reach)
    padded_re = jnp.pad(field_re, widths)
    padded_im = jnp.pad(field_im, widths)
    out_re = jnp.zeros_like(field_re)
    out_im = jnp.zeros_like(field_im)
    for offset in range(2 * reach + 1):
        anchor = 2 * reach - offset if adjoint else offset
        shifted_re = lax.slice_in_dim(padded_re, anchor, anchor + extent, axis=along)
        shifted_im = lax.slice_in_dim(padded_im, anchor, anchor + extent, axis=along)
        coef_re = tap_re[..., offset][..., None, None]
        coef_im = tap_im[..., offset][..., None, None]
        if adjoint:
            out_re = out_re + coef_re * shifted_re + coef_im * shifted_im
            out_im = out_im + coef_re * shifted_im - coef_im * shifted_re
        else:
            out_re = out_re + coef_re * shifted_re - coef_im * shifted_im
            out_im = out_im + coef_re * shifted_im + coef_im * shifted_re
    return out_re, out_im


def forward_step(field_re, field_im, tap_re, tap_im, phase_cos, phase_sin):
    mid_re, mid_im = convolve(field_re, field_im, tap_re, tap_im, -1, False)
    mid_re, mid_im = convolve(mid_re, mid_im, tap_re, tap_im, -2, False)
    return phase_cos * mid_re - phase_sin * mid_im, phase_sin * mid_re + phase_cos * mid_im


def adjoint_step(field_re, field_im, tap_re, tap_im, phase_cos, phase_sin):
    mid_re = phase_cos * field_re + phase_sin * field_im
    mid_im = phase_cos * field_im - phase_sin * field_re
    mid_re, mid_im = convolve(mid_re, mid_im, tap_re, tap_im, -2, True)
    return convolve(mid_re, mid_im, tap_re, tap_im, -1, True)


def reference(slowness, freq_index, taps, source_top, adjoint_source):
    sections = source_top.shape[1]
    depth_total = slowness.shape[0]
    steps = depth_total // sections
    lines, cells = source_top.shape[3], source_top.shape[4]
    slow_grid = slowness.reshape(depth_total, lines, cells)
    count = taps.shape[0]

    def per_freq(total, inputs):
        index, source, adjoint = inputs
        angular = 8.0 * (index.astype(jnp.float32) + 1.0) / count
        tap_row = taps[index]
        tap_re, tap_im = tap_row[0], tap_row[1]
        phase = angular * slow_grid
        phase_cos = jnp.cos(phase)
        phase_sin = jnp.sin(phase)
        cos_sec = phase_cos.reshape(sections, steps, lines, cells)
        sin_sec = phase_sin.reshape(sections, steps, lines, cells)
        field_re, field_im = source[:, 0], source[:, 1]
        waves_re, waves_im = [], []
        for step in range(steps):
            field_re, field_im = forward_step(field_re, field_im, tap_re, tap_im, cos_sec[:, step], sin_sec[:, step])
            waves_re.append(field_re)
            waves_im.append(field_im)
        wave_re = jnp.stack(waves_re, axis=1).reshape(depth_total, lines, cells)
        wave_im = jnp.stack(waves_im, axis=1).reshape(depth_total, lines, cells)

        def backward(incoming, xs):
            q_re, q_im, w_re, w_im, c_part, s_part = xs
            mu_re = q_re + incoming[0]
            mu_im = q_im + incoming[1]
            term = angular * (mu_im * w_re - mu_re * w_im)
            return adjoint_step(mu_re, mu_im, tap_re, tap_im, c_part, s_part), term

        start = (jnp.zeros((lines, cells), jnp.float32), jnp.zeros((lines, cells), jnp.float32))
        _, terms = lax.scan(backward, start, (adjoint[:, 0], adjoint[:, 1], wave_re, wave_im, phase_cos, phase_sin), reverse=True)
        return total + terms, None

    total, _ = lax.scan(per_freq, jnp.zeros((depth_total, lines, cells), jnp.float32), (freq_index, source_top, adjoint_source))
    return (total / count).reshape(depth_total, lines * cells)
```

```python
import functools
import math

import jax
import jax.numpy as jnp
from jax import lax
from jax.experimental import pallas as pl
from jax.experimental.pallas import tpu as pltpu
from jax.sharding import PartitionSpec as P

MESH = pl.DeviceIdType.MESH
LANES = 128
SUB = 8
BLOCK = 4
CHUNK = 8

PI_HIGH = 3.140625
PI_LOW = math.pi - PI_HIGH


def sin_cos(phase):
    turns = jnp.floor(phase * (1.0 / math.pi) + 0.5)
    rest = (phase - turns * PI_HIGH) - turns * PI_LOW
    sign = 1.0 - 2.0 * (turns - 2.0 * jnp.floor(turns * 0.5))
    square = rest * rest
    odd = -1.0 / math.factorial(11)
    for n, s in ((9, 1), (7, -1), (5, 1), (3, -1), (1, 1)):
        odd = odd * square + s / math.factorial(n)
    even = 1.0 / math.factorial(12)
    for n, s in ((10, -1), (8, 1), (6, -1), (4, 1), (2, -1), (0, 1)):
        even = even * square + s / math.factorial(n)
    return sign * rest * odd, sign * even


def shifted(value, reach):
    lane = lax.broadcasted_iota(jnp.int32, value.shape, 2)
    row = lax.broadcasted_iota(jnp.int32, value.shape, 1)
    after = jnp.where(row < SUB - 1, pltpu.roll(value, SUB - 1, 1), 0.0)
    before = jnp.where(row > 0, pltpu.roll(value, 1, 1), 0.0)
    out = {0: value}
    for o in range(1, reach + 1):
        out[o] = pltpu.roll(jnp.where(lane >= o, value, after), LANES - o, 2)
        out[-o] = pltpu.roll(jnp.where(lane < LANES - o, value, before), o, 2)
    return out


def filtered(at_re, at_im, taps, adjoint):
    reach = len(taps) // 2
    out_re = out_im = None
    for k, (t_re, t_im) in enumerate(taps):
        o = reach - k if adjoint else k - reach
        u_re, u_im = at_re(o), at_im(o)
        if adjoint:
            t_im = -t_im
        add_re = t_re * u_re - t_im * u_im
        add_im = t_re * u_im + t_im * u_re
        out_re = add_re if out_re is None else out_re + add_re
        out_im = add_im if out_im is None else out_im + add_im
    return out_re, out_im


def filter_x(re, im, taps, adjoint):
    reach = len(taps) // 2
    all_re, all_im = shifted(re, reach), shifted(im, reach)
    return filtered(lambda o: all_re[o], lambda o: all_im[o], taps, adjoint)


def kernel(
    peers, depths, lanes, lines, reach, count, per_piece, whole_lines,
    slow_ref, index_ref, taps_ref, source_ref, adjoint_ref, out_ref,
    source_in, adjoint_in, wave, adj, padded, slow, cosine, sine,
    arrived, leaving, grad, gathered,
    in_sem, slow_send, slow_recv, mu_send, mu_recv, grad_send, grad_recv,
):
    me = lax.axis_index("freq")
    d = lax.axis_index("depth")
    chunks = lines // CHUNK

    load_source = pltpu.make_async_copy(source_ref, source_in, in_sem.at[0])
    load_adjoint = pltpu.make_async_copy(adjoint_ref, adjoint_in, in_sem.at[1])
    load_source.start()
    load_adjoint.start()

    barrier = pltpu.get_barrier_semaphore()

    def peer(i):
        return lax.rem(me + i, peers)

    def greet(i, carry):
        pl.semaphore_signal(barrier, inc=1, device_id={"freq": peer(i)}, device_id_type=MESH)
        return carry

    lax.fori_loop(1, peers, greet, 0)

    @pl.when(d < depths - 1)
    def _():
        pl.semaphore_signal(barrier, inc=1, device_id={"depth": d + 1}, device_id_type=MESH)

    def piece(i):
        return pl.ds(i * per_piece, per_piece)

    slow[piece(me)] = slow_ref[...]
    margin = jnp.zeros((reach, SUB, LANES), jnp.float32)
    for part in range(2):
        padded[part, pl.ds(0, reach)] = margin
        padded[part, pl.ds(lines + reach, reach)] = margin
    grad[...] = jnp.zeros_like(grad)

    @pl.when(d == depths - 1)
    def _():
        arrived[...] = jnp.zeros_like(arrived)

    pl.semaphore_wait(barrier, jnp.where(d > 0, peers, peers - 1))

    def send_slow(i):
        return pltpu.make_async_remote_copy(
            src_ref=slow_ref, dst_ref=slow.at[piece(me)],
            send_sem=slow_send.at[peer(i)], recv_sem=slow_recv.at[me],
            device_id={"freq": peer(i)}, device_id_type=MESH,
        )

    def recv_slow(i):
        return pltpu.make_async_remote_copy(
            src_ref=slow_ref, dst_ref=slow.at[piece(peer(i))],
            send_sem=slow_send.at[peer(i)], recv_sem=slow_recv.at[peer(i)],
            device_id={"freq": peer(i)}, device_id_type=MESH,
        )

    def start_slow(i, carry):
        send_slow(i).start()
        return carry

    lax.fori_loop(1, peers, start_slow, 0)

    def tap_list(f):
        row = index_ref[f]
        return [(taps_ref[k, 0, row], taps_ref[k, 1, row]) for k in range(2 * reach + 1)]

    def angular(f):
        return 8.0 * (index_ref[f].astype(jnp.float32) + 1.0) / count

    def blocks(y, n=BLOCK):
        return pl.ds(y, n)

    def unfold(from_ref, to_ref):
        def body(i, carry):
            f, part = i // 2, i % 2
            for t in range(lines // SUB):
                rows = from_ref[f, part, pl.ds(t * SUB, SUB), :]
                to_ref[f, part, pl.ds(t * SUB, SUB)] = rows.reshape(SUB, SUB, LANES)
            return carry

        lax.fori_loop(0, 2 * lanes, body, 0)

    def filter_y(y, taps, adjoint):
        return filtered(
            lambda o: padded[0, blocks(y + reach + o)],
            lambda o: padded[1, blocks(y + reach + o)],
            taps, adjoint,
        )

    load_source.wait()
    unfold(source_in, wave)

    def forward(f, carry):
        taps = tap_list(f)

        def along_x(b, c):
            y = b * BLOCK
            re, im = filter_x(wave[f, 0, blocks(y)], wave[f, 1, blocks(y)], taps, False)
            padded[0, blocks(y + reach)] = re
            padded[1, blocks(y + reach)] = im
            return c

        def along_y(b, c):
            y = b * BLOCK
            re, im = filter_y(y, taps, False)
            wave[f, 0, blocks(y)] = re
            wave[f, 1, blocks(y)] = im
            return c

        lax.fori_loop(0, lines // BLOCK, along_x, 0)
        lax.fori_loop(0, lines // BLOCK, along_y, 0)
        return carry

    lax.fori_loop(0, lanes, forward, 0)

    load_adjoint.wait()
    unfold(adjoint_in, adj)

    def wait_slow(i, carry):
        recv_slow(i).wait_recv()
        return carry

    lax.fori_loop(1, peers, wait_slow, 0)

    def slow_block(y):
        if whole_lines:
            return slow[blocks(y)]
        per_line = SUB * peers // (lines * SUB)
        return slow[pl.ds(y * per_line, BLOCK * per_line)].reshape(BLOCK, SUB, LANES)

    def phases(f, carry):
        w = angular(f)

        def body(b, c):
            y = b * BLOCK
            s, co = sin_cos(w * slow_block(y))
            sine[f, blocks(y)] = s
            cosine[f, blocks(y)] = co
            re, im = wave[f, 0, blocks(y)], wave[f, 1, blocks(y)]
            wave[f, 0, blocks(y)] = w * (co * re - s * im)
            wave[f, 1, blocks(y)] = w * (s * re + co * im)
            return c

        lax.fori_loop(0, lines // BLOCK, body, 0)
        return carry

    lax.fori_loop(0, lanes, phases, 0)

    def hop(f, chunk):
        rows = pl.ds(chunk * CHUNK, CHUNK)
        slot = f * chunks + chunk
        return pltpu.make_async_remote_copy(
            src_ref=leaving.at[f, rows], dst_ref=arrived.at[f, rows],
            send_sem=mu_send.at[slot], recv_sem=mu_recv.at[slot],
            device_id={"depth": lax.max(d - 1, 0)}, device_id_type=MESH,
        )

    def add_grad(y, term):
        if whole_lines:
            grad[blocks(y)] += term
        else:
            per_line = SUB * peers // (lines * SUB)
            grad[pl.ds(y * per_line, BLOCK * per_line)] += term.reshape(
                BLOCK * per_line, SUB // per_line, LANES
            )

    def chain(f, carry):
        taps = tap_list(f)

        def take(chunk):
            @pl.when(d < depths - 1)
            def _():
                hop(f, chunk).wait_recv()

            def body(b, c):
                y = chunk * CHUNK + b * BLOCK
                mu_re = adj[f, 0, blocks(y)] + arrived[f, blocks(y), 0]
                mu_im = adj[f, 1, blocks(y)] + arrived[f, blocks(y), 1]
                add_grad(y, mu_im * wave[f, 0, blocks(y)] - mu_re * wave[f, 1, blocks(y)])
                co, s = cosine[f, blocks(y)], sine[f, blocks(y)]
                padded[0, blocks(y + reach)] = co * mu_re + s * mu_im
                padded[1, blocks(y + reach)] = co * mu_im - s * mu_re
                return c

            lax.fori_loop(0, CHUNK // BLOCK, body, 0)

        def give(chunk):
            @pl.when(d > 0)
            def _():
                def body(b, c):
                    y = chunk * CHUNK + b * BLOCK
                    re, im = filter_y(y, taps, True)
                    re, im = filter_x(re, im, taps, True)
                    leaving[f, blocks(y), 0] = re
                    leaving[f, blocks(y), 1] = im
                    return c

                lax.fori_loop(0, CHUNK // BLOCK, body, 0)
                hop(f, chunk).start()

        for chunk in range(chunks):
            take(chunk)
            if chunk > 0:
                give(chunk - 1)
        give(chunks - 1)
        return carry

    lax.fori_loop(0, lanes, chain, 0)

    def send_grad(i):
        return pltpu.make_async_remote_copy(
            src_ref=grad.at[piece(peer(i))], dst_ref=gathered.at[me],
            send_sem=grad_send.at[peer(i)], recv_sem=grad_recv.at[me],
            device_id={"freq": peer(i)}, device_id_type=MESH,
        )

    def recv_grad(i):
        return pltpu.make_async_remote_copy(
            src_ref=grad.at[piece(peer(i))], dst_ref=gathered.at[peer(i)],
            send_sem=grad_send.at[peer(i)], recv_sem=grad_recv.at[peer(i)],
            device_id={"freq": peer(i)}, device_id_type=MESH,
        )

    def start_grad(i, carry):
        send_grad(i).start()
        return carry

    lax.fori_loop(1, peers, start_grad, 0)
    gathered[me] = grad[piece(me)]

    def wait_grad(i, carry):
        recv_grad(i).wait_recv()
        return carry

    lax.fori_loop(1, peers, wait_grad, 0)

    def add(i, total):
        return total + gathered[i]

    total = lax.fori_loop(0, peers, add, jnp.zeros(out_ref.shape, jnp.float32))
    out_ref[...] = total * (1.0 / count)

    def drain(i, carry):
        send_slow(i).wait_send()
        send_grad(i).wait_send()
        return carry

    lax.fori_loop(1, peers, drain, 0)

    @pl.when(d > 0)
    def _():
        def drain_mu(i, carry):
            hop(i // chunks, i % chunks).wait_send()
            return carry

        lax.fori_loop(0, lanes * chunks, drain_mu, 0)


def on_device(slowness, freq_index, taps, source_top, adjoint_source):
    lanes, _, _, lines, cells = source_top.shape
    peers, depths = lax.axis_size("freq"), lax.axis_size("depth")
    count, _, width = taps.shape
    reach = width // 2
    assert cells == SUB * LANES and slowness.shape[0] == 1
    rows = slowness.shape[1] // LANES
    whole_lines = rows % SUB == 0
    piece = (rows // SUB, SUB, LANES) if whole_lines else (1, rows, LANES)
    pieces = (piece[0] * peers,) + piece[1:]
    line = (SUB, LANES)
    f32 = jnp.float32
    vmem = pl.BlockSpec(memory_space=pltpu.VMEM)
    smem = pl.BlockSpec(memory_space=pltpu.SMEM)
    hbm = pl.BlockSpec(memory_space=pl.ANY)
    dma = pltpu.SemaphoreType.DMA
    chunks = lines // CHUNK
    out = pl.pallas_call(
        functools.partial(
            kernel, peers, depths, lanes, lines, reach, count, piece[0], whole_lines
        ),
        out_shape=jax.ShapeDtypeStruct(piece, f32),
        in_specs=[vmem, smem, smem, hbm, hbm],
        out_specs=vmem,
        scratch_shapes=[
            pltpu.VMEM((lanes, 2, lines, cells), f32),
            pltpu.VMEM((lanes, 2, lines, cells), f32),
            pltpu.VMEM((lanes, 2, lines) + line, f32),
            pltpu.VMEM((lanes, 2, lines) + line, f32),
            pltpu.VMEM((2, lines + 2 * reach) + line, f32),
            pltpu.VMEM(pieces, f32),
            pltpu.VMEM((lanes, lines) + line, f32),
            pltpu.VMEM((lanes, lines) + line, f32),
            pltpu.VMEM((lanes, lines, 2) + line, f32),
            pltpu.VMEM((lanes, lines, 2) + line, f32),
            pltpu.VMEM(pieces, f32),
            pltpu.VMEM((peers,) + piece, f32),
            dma((2,)),
            dma((peers,)),
            dma((peers,)),
            dma((lanes * chunks,)),
            dma((lanes * chunks,)),
            dma((peers,)),
            dma((peers,)),
        ],
        compiler_params=pltpu.CompilerParams(
            collective_id=0, has_side_effects=True, vmem_limit_bytes=56 * 1024 * 1024
        ),
    )(
        slowness.reshape(piece),
        freq_index,
        taps.transpose(2, 1, 0),
        source_top.reshape(lanes, 2, lines, cells),
        adjoint_source.reshape(lanes, 2, lines, cells),
    )
    return out.reshape(slowness.shape)


def solution(mesh):
    in_specs = (
        P("depth", "freq"),
        P("freq"),
        P(),
        P("freq", "depth", None, None, None),
        P("freq", "depth", None, None, None),
    )
    out_specs = P("depth", "freq")
    return jax.shard_map(
        on_device, mesh=mesh, in_specs=in_specs, out_specs=out_specs, check_vma=False
    )
```

```python
import functools
import math

import jax
import jax.numpy as jnp
from jax import lax
from jax.experimental import pallas as pl
from jax.experimental.pallas import tpu as pltpu
from jax.sharding import PartitionSpec as P

MESH = pl.DeviceIdType.MESH
LANES = 128
SUB = 8
BLOCK = 4
CHUNK = 8

PI_HIGH = 3.140625
PI_LOW = math.pi - PI_HIGH


def sin_cos(phase):
    turns = jnp.floor(phase * (1.0 / math.pi) + 0.5)
    rest = (phase - turns * PI_HIGH) - turns * PI_LOW
    sign = 1.0 - 2.0 * (turns - 2.0 * jnp.floor(turns * 0.5))
    square = rest * rest
    odd = -1.0 / math.factorial(11)
    for n, s in ((9, 1), (7, -1), (5, 1), (3, -1), (1, 1)):
        odd = odd * square + s / math.factorial(n)
    even = 1.0 / math.factorial(12)
    for n, s in ((10, -1), (8, 1), (6, -1), (4, 1), (2, -1), (0, 1)):
        even = even * square + s / math.factorial(n)
    return sign * rest * odd, sign * even


def shifted(value, reach):
    lane = lax.broadcasted_iota(jnp.int32, value.shape, 2)
    row = lax.broadcasted_iota(jnp.int32, value.shape, 1)
    after = jnp.where(row < SUB - 1, pltpu.roll(value, SUB - 1, 1), 0.0)
    before = jnp.where(row > 0, pltpu.roll(value, 1, 1), 0.0)
    out = {0: value}
    for o in range(1, reach + 1):
        out[o] = pltpu.roll(jnp.where(lane >= o, value, after), LANES - o, 2)
        out[-o] = pltpu.roll(jnp.where(lane < LANES - o, value, before), o, 2)
    return out


def filtered(at_re, at_im, taps, adjoint):
    reach = len(taps) // 2
    out_re = out_im = None
    for k, (t_re, t_im) in enumerate(taps):
        o = reach - k if adjoint else k - reach
        u_re, u_im = at_re(o), at_im(o)
        if adjoint:
            t_im = -t_im
        add_re = t_re * u_re - t_im * u_im
        add_im = t_re * u_im + t_im * u_re
        out_re = add_re if out_re is None else out_re + add_re
        out_im = add_im if out_im is None else out_im + add_im
    return out_re, out_im


def filter_x(re, im, taps, adjoint):
    reach = len(taps) // 2
    all_re, all_im = shifted(re, reach), shifted(im, reach)
    return filtered(lambda o: all_re[o], lambda o: all_im[o], taps, adjoint)


def kernel(
    peers, depths, lanes, lines, reach, count, per_piece, whole_lines,
    slow_hbm, index_hbm, taps_hbm, source_hbm, adjoint_hbm, out_ref,
    slow_ref, index_ref, taps_ref, source_in, adjoint_in, wave, adj, padded, slow, cosine, sine,
    arrived, leaving, grad, gathered,
    in_sem, slow_send, slow_recv, mu_send, mu_recv, grad_send, grad_recv,
):
    me = lax.axis_index("freq")
    d = lax.axis_index("depth")
    chunks = lines // CHUNK
    per_line = max(1, peers // lines)

    load_slow = pltpu.make_async_copy(slow_hbm, slow_ref, in_sem.at[0])
    load_index = pltpu.make_async_copy(index_hbm, index_ref, in_sem.at[1])
    load_taps = pltpu.make_async_copy(taps_hbm, taps_ref, in_sem.at[2])
    load_adjoint = pltpu.make_async_copy(adjoint_hbm, adjoint_in, in_sem.at[3])
    load_source = pltpu.make_async_copy(source_hbm, source_in, in_sem.at[4])

    barrier = pltpu.get_barrier_semaphore()

    def peer(i):
        return lax.rem(me + i, peers)

    def greet(i, carry):
        pl.semaphore_signal(barrier, inc=1, device_id={"freq": peer(i)}, device_id_type=MESH)
        return carry

    lax.fori_loop(1, peers, greet, 0)

    @pl.when(d < depths - 1)
    def _():
        pl.semaphore_signal(barrier, inc=1, device_id={"depth": d + 1}, device_id_type=MESH)

    for load in (load_slow, load_index, load_taps, load_adjoint, load_source):
        load.start()

    def piece(i):
        return pl.ds(i * per_piece, per_piece)

    margin = jnp.zeros((reach, SUB, LANES), jnp.float32)
    for part in range(2):
        padded[part, pl.ds(0, reach)] = margin
        padded[part, pl.ds(lines + reach, reach)] = margin
    grad[...] = jnp.zeros_like(grad)

    @pl.when(d == depths - 1)
    def _():
        arrived[...] = jnp.zeros_like(arrived)

    load_slow.wait()
    slow[piece(me)] = slow_ref[...]
    pl.semaphore_wait(barrier, jnp.where(d > 0, peers, peers - 1))

    def push_slow(i, sender):
        return pltpu.make_async_remote_copy(
            src_ref=slow_ref, dst_ref=slow.at[piece(sender)],
            send_sem=slow_send.at[peer(i)], recv_sem=slow_recv.at[sender],
            device_id={"freq": peer(i)}, device_id_type=MESH,
        )

    def start_slow(i, carry):
        push_slow(i, me).start()
        return carry

    lax.fori_loop(1, peers, start_slow, 0)
    load_index.wait()
    load_taps.wait()

    def wait_slow(i, carry):
        push_slow(i, peer(i)).wait_recv()
        return carry

    def tap_list(f):
        row = index_ref[f]
        return [(taps_ref[k, 0, row], taps_ref[k, 1, row]) for k in range(2 * reach + 1)]

    def angular(f):
        return 8.0 * (index_ref[f].astype(jnp.float32) + 1.0) / count

    def block(y):
        return pl.ds(y, BLOCK)

    def each_block(first, last, body):
        def step(b, carry):
            body(b * BLOCK)
            return carry

        lax.fori_loop(first // BLOCK, last // BLOCK, step, 0)

    def each_lane(body):
        def step(f, carry):
            body(f)
            return carry

        lax.fori_loop(0, lanes, step, 0)

    def unfold(from_ref, to_ref):
        def body(i, carry):
            f, part = i // 2, i % 2
            for t in range(lines // SUB):
                rows = from_ref[f, part, pl.ds(t * SUB, SUB), :]
                to_ref[f, part, pl.ds(t * SUB, SUB)] = rows.reshape(SUB, SUB, LANES)
            return carry

        lax.fori_loop(0, 2 * lanes, body, 0)

    def filter_y(y, taps, adjoint):
        return filtered(
            lambda o: padded[0, block(y + reach + o)],
            lambda o: padded[1, block(y + reach + o)],
            taps, adjoint,
        )

    def slow_block(y):
        if whole_lines:
            return slow[block(y)]
        return slow[pl.ds(y * per_line, BLOCK * per_line)].reshape(BLOCK, SUB, LANES)

    def add_grad(y, term):
        if whole_lines:
            grad[block(y)] += term
        else:
            grad[pl.ds(y * per_line, BLOCK * per_line)] += term.reshape(
                BLOCK * per_line, SUB // per_line, LANES
            )

    def phases(f):
        w = angular(f)

        def body(y):
            s, co = sin_cos(w * slow_block(y))
            sine[f, block(y)] = s
            cosine[f, block(y)] = co

        each_block(0, lines, body)

    def forward(f, finish):
        taps = tap_list(f)

        def along_x(y):
            re, im = filter_x(wave[f, 0, block(y)], wave[f, 1, block(y)], taps, False)
            padded[0, block(y + reach)] = re
            padded[1, block(y + reach)] = im

        def along_y(y):
            finish(f, y, *filter_y(y, taps, False))

        each_block(0, lines, along_x)
        each_block(0, lines, along_y)

    def turned(f, y, re, im):
        w, co, s = angular(f), cosine[f, block(y)], sine[f, block(y)]
        return w * (co * re - s * im), w * (s * re + co * im)

    def hop(f, chunk):
        rows = pl.ds(chunk * CHUNK, CHUNK)
        slot = f * chunks + chunk
        return pltpu.make_async_remote_copy(
            src_ref=leaving.at[f, rows], dst_ref=arrived.at[f, rows],
            send_sem=mu_send.at[slot], recv_sem=mu_recv.at[slot],
            device_id={"depth": lax.max(d - 1, 0)}, device_id_type=MESH,
        )

    def chain(f, use):
        taps = tap_list(f)

        def take(chunk):
            @pl.when(d < depths - 1)
            def _():
                hop(f, chunk).wait_recv()

            def body(y):
                mu_re = adj[f, 0, block(y)] + arrived[f, block(y), 0]
                mu_im = adj[f, 1, block(y)] + arrived[f, block(y), 1]
                use(f, y, mu_re, mu_im)
                co, s = cosine[f, block(y)], sine[f, block(y)]
                padded[0, block(y + reach)] = co * mu_re + s * mu_im
                padded[1, block(y + reach)] = co * mu_im - s * mu_re

            each_block(chunk * CHUNK, (chunk + 1) * CHUNK, body)

        def give(chunk):
            @pl.when(d > 0)
            def _():
                def body(y):
                    re, im = filter_y(y, taps, True)
                    re, im = filter_x(re, im, taps, True)
                    leaving[f, block(y), 0] = re
                    leaving[f, block(y), 1] = im

                each_block(chunk * CHUNK, (chunk + 1) * CHUNK, body)
                hop(f, chunk).start()

        for chunk in range(chunks):
            take(chunk)
            if chunk > 0:
                give(chunk - 1)
        give(chunks - 1)

    def push_grad(to, sender):
        return pltpu.make_async_remote_copy(
            src_ref=grad.at[piece(to)], dst_ref=gathered.at[sender],
            send_sem=grad_send.at[to], recv_sem=grad_recv.at[sender],
            device_id={"freq": to}, device_id_type=MESH,
        )

    def send_grad(first, last):
        def step(to, carry):
            @pl.when(to != me)
            def _():
                push_grad(to, me).start()

            return carry

        lax.fori_loop(first, last, step, 0)

    early = d >= depths // 2

    @pl.when(early)
    def _():
        load_adjoint.wait()
        unfold(adjoint_in, adj)
        lax.fori_loop(1, peers, wait_slow, 0)

        def keep(f, y, mu_re, mu_im):
            adj[f, 0, block(y)] = mu_re
            adj[f, 1, block(y)] = mu_im

        def first(f):
            phases(f)
            chain(f, keep)

        each_lane(first)
        load_source.wait()
        unfold(source_in, wave)

        def finish(f, y, re, im):
            re, im = turned(f, y, re, im)
            add_grad(y, adj[f, 1, block(y)] * re - adj[f, 0, block(y)] * im)

        each_lane(lambda f: forward(f, finish))
        send_grad(0, peers)

    @pl.when(jnp.logical_not(early))
    def _():
        load_source.wait()
        unfold(source_in, wave)

        def finish(f, y, re, im):
            wave[f, 0, block(y)] = re
            wave[f, 1, block(y)] = im

        each_lane(lambda f: forward(f, finish))
        load_adjoint.wait()
        unfold(adjoint_in, adj)
        lax.fori_loop(1, peers, wait_slow, 0)

        def turn(f):
            phases(f)

            def body(y):
                re, im = turned(f, y, wave[f, 0, block(y)], wave[f, 1, block(y)])
                wave[f, 0, block(y)] = re
                wave[f, 1, block(y)] = im

            each_block(0, lines, body)

        each_lane(turn)

        def use(f, y, mu_re, mu_im):
            add_grad(y, mu_im * wave[f, 0, block(y)] - mu_re * wave[f, 1, block(y)])

        each_lane(lambda f: chain(f, use))
        send_grad(0, peers)

    gathered[me] = grad[piece(me)]

    def add(i, total):
        push_grad(me, peer(i)).wait_recv()
        return total + gathered[peer(i)]

    total = lax.fori_loop(1, peers, add, gathered[me])
    out_ref[...] = total * (1.0 / count)

    def drain(i, carry):
        push_slow(i, me).wait_send()
        push_grad(peer(i), me).wait_send()
        return carry

    lax.fori_loop(1, peers, drain, 0)

    @pl.when(d > 0)
    def _():
        def drain_mu(i, carry):
            hop(i // chunks, i % chunks).wait_send()
            return carry

        lax.fori_loop(0, lanes * chunks, drain_mu, 0)


def on_device(slowness, freq_index, taps, source_top, adjoint_source):
    lanes, _, _, lines, cells = source_top.shape
    peers, depths = lax.axis_size("freq"), lax.axis_size("depth")
    count, _, width = taps.shape
    reach = width // 2
    assert cells == SUB * LANES and slowness.shape[0] == 1
    rows = slowness.shape[1] // LANES
    whole_lines = rows % SUB == 0
    piece = (rows // SUB, SUB, LANES) if whole_lines else (1, rows, LANES)
    pieces = (piece[0] * peers,) + piece[1:]
    line = (SUB, LANES)
    f32 = jnp.float32
    vmem = pl.BlockSpec(memory_space=pltpu.VMEM)
    hbm = pl.BlockSpec(memory_space=pl.ANY)
    dma = pltpu.SemaphoreType.DMA
    chunks = lines // CHUNK
    out = pl.pallas_call(
        functools.partial(
            kernel, peers, depths, lanes, lines, reach, count, piece[0], whole_lines
        ),
        out_shape=jax.ShapeDtypeStruct(piece, f32),
        in_specs=[hbm] * 5,
        out_specs=vmem,
        scratch_shapes=[
            pltpu.VMEM(piece, f32),
            pltpu.SMEM((lanes,), jnp.int32),
            pltpu.SMEM((width, 2, count), f32),
            pltpu.VMEM((lanes, 2, lines, cells), f32),
            pltpu.VMEM((lanes, 2, lines, cells), f32),
            pltpu.VMEM((lanes, 2, lines) + line, f32),
            pltpu.VMEM((lanes, 2, lines) + line, f32),
            pltpu.VMEM((2, lines + 2 * reach) + line, f32),
            pltpu.VMEM(pieces, f32),
            pltpu.VMEM((lanes, lines) + line, f32),
            pltpu.VMEM((lanes, lines) + line, f32),
            pltpu.VMEM((lanes, lines, 2) + line, f32),
            pltpu.VMEM((lanes, lines, 2) + line, f32),
            pltpu.VMEM(pieces, f32),
            pltpu.VMEM((peers,) + piece, f32),
            dma((5,)),
            dma((peers,)),
            dma((peers,)),
            dma((lanes * chunks,)),
            dma((lanes * chunks,)),
            dma((peers,)),
            dma((peers,)),
        ],
        compiler_params=pltpu.CompilerParams(
            collective_id=0, has_side_effects=True, vmem_limit_bytes=56 * 1024 * 1024
        ),
    )(
        slowness.reshape(piece),
        freq_index,
        taps.transpose(2, 1, 0),
        source_top.reshape(lanes, 2, lines, cells),
        adjoint_source.reshape(lanes, 2, lines, cells),
    )
    return out.reshape(slowness.shape)


def solution(mesh):
    in_specs = (
        P("depth", "freq"),
        P("freq"),
        P(),
        P("freq", "depth", None, None, None),
        P("freq", "depth", None, None, None),
    )
    out_specs = P("depth", "freq")
    return jax.shard_map(
        on_device, mesh=mesh, in_specs=in_specs, out_specs=out_specs, check_vma=False
    )
```

```python
import functools
import math

import jax
import jax.numpy as jnp
from jax import lax
from jax.experimental import pallas as pl
from jax.experimental.pallas import tpu as pltpu
from jax.sharding import PartitionSpec as P

MESH = pl.DeviceIdType.MESH
LANES = 128
SUB = 8
BLOCK = 4
CHUNK = 8

PI_HIGH = 3.140625
PI_LOW = math.pi - PI_HIGH


def sin_cos(phase):
    turns = jnp.floor(phase * (1.0 / math.pi) + 0.5)
    rest = (phase - turns * PI_HIGH) - turns * PI_LOW
    sign = 1.0 - 2.0 * (turns - 2.0 * jnp.floor(turns * 0.5))
    square = rest * rest
    odd = -1.0 / math.factorial(11)
    for n, s in ((9, 1), (7, -1), (5, 1), (3, -1), (1, 1)):
        odd = odd * square + s / math.factorial(n)
    even = 1.0 / math.factorial(12)
    for n, s in ((10, -1), (8, 1), (6, -1), (4, 1), (2, -1), (0, 1)):
        even = even * square + s / math.factorial(n)
    return sign * rest * odd, sign * even


def shifted(value, reach):
    lane = lax.broadcasted_iota(jnp.int32, value.shape, 2)
    row = lax.broadcasted_iota(jnp.int32, value.shape, 1)
    after = jnp.where(row < SUB - 1, pltpu.roll(value, SUB - 1, 1), 0.0)
    before = jnp.where(row > 0, pltpu.roll(value, 1, 1), 0.0)
    out = {0: value}
    for o in range(1, reach + 1):
        out[o] = pltpu.roll(jnp.where(lane >= o, value, after), LANES - o, 2)
        out[-o] = pltpu.roll(jnp.where(lane < LANES - o, value, before), o, 2)
    return out


def filtered(at, taps, adjoint):
    reach = len(taps) // 2
    total = None
    for k, (t_re, t_im) in enumerate(taps):
        o = reach - k if adjoint else k - reach
        u_re, u_im, u_sum = at(o)
        if adjoint:
            t_im = -t_im
        new = (t_re * u_sum, (t_im - t_re) * u_re, (t_re + t_im) * u_im)
        total = new if total is None else tuple(x + y for x, y in zip(total, new))
    a, b, c = total
    return a - c, a + b


def filter_x(re, im, taps, adjoint):
    reach = len(taps) // 2
    all_re, all_im = shifted(re, reach), shifted(im, reach)
    return filtered(lambda o: (all_re[o], all_im[o], all_re[o] + all_im[o]), taps, adjoint)


def kernel(
    peers, depths, lanes, lines, reach, count, per_piece, whole_lines,
    slow_hbm, index_hbm, taps_hbm, source_hbm, adjoint_hbm, out_ref,
    slow_ref, index_ref, taps_ref, source_in, adjoint_in, wave, adj, padded, slow, cosine, sine,
    arrived, leaving, grad, gathered,
    in_sem, slow_send, slow_recv, mu_send, mu_recv, grad_send, grad_recv,
):
    me = lax.axis_index("freq")
    d = lax.axis_index("depth")
    chunks = lines // CHUNK
    per_line = max(1, peers // lines)

    load_slow = pltpu.make_async_copy(slow_hbm, slow_ref, in_sem.at[0])
    load_index = pltpu.make_async_copy(index_hbm, index_ref, in_sem.at[1])
    load_taps = pltpu.make_async_copy(taps_hbm, taps_ref, in_sem.at[2])
    load_adjoint = pltpu.make_async_copy(adjoint_hbm, adjoint_in, in_sem.at[3])
    load_source = pltpu.make_async_copy(source_hbm, source_in, in_sem.at[4])

    barrier = pltpu.get_barrier_semaphore()

    def peer(i):
        return lax.rem(me + i, peers)

    def greet(i, carry):
        pl.semaphore_signal(barrier, inc=1, device_id={"freq": peer(i)}, device_id_type=MESH)
        return carry

    lax.fori_loop(1, peers, greet, 0)

    @pl.when(d < depths - 1)
    def _():
        pl.semaphore_signal(barrier, inc=1, device_id={"depth": d + 1}, device_id_type=MESH)

    for load in (load_slow, load_index, load_taps, load_adjoint, load_source):
        load.start()

    def piece(i):
        return pl.ds(i * per_piece, per_piece)

    margin = jnp.zeros((reach, SUB, LANES), jnp.float32)
    for part in range(3):
        padded[part, pl.ds(0, reach)] = margin
        padded[part, pl.ds(lines + reach, reach)] = margin
    grad[...] = jnp.zeros_like(grad)

    @pl.when(d == depths - 1)
    def _():
        arrived[...] = jnp.zeros_like(arrived)

    load_slow.wait()
    slow[piece(me)] = slow_ref[...]
    pl.semaphore_wait(barrier, jnp.where(d > 0, peers, peers - 1))

    def push_slow(i, sender):
        return pltpu.make_async_remote_copy(
            src_ref=slow_ref, dst_ref=slow.at[piece(sender)],
            send_sem=slow_send.at[peer(i)], recv_sem=slow_recv.at[sender],
            device_id={"freq": peer(i)}, device_id_type=MESH,
        )

    def start_slow(i, carry):
        push_slow(i, me).start()
        return carry

    lax.fori_loop(1, peers, start_slow, 0)
    load_index.wait()
    load_taps.wait()

    def wait_slow(i, carry):
        push_slow(i, peer(i)).wait_recv()
        return carry

    def tap_list(f):
        row = index_ref[f]
        return [(taps_ref[k, 0, row], taps_ref[k, 1, row]) for k in range(2 * reach + 1)]

    def angular(f):
        return 8.0 * (index_ref[f].astype(jnp.float32) + 1.0) / count

    def block(y):
        return pl.ds(y, BLOCK)

    def each_block(first, last, body):
        def step(b, carry):
            for part in range(CHUNK // BLOCK):
                body(b * CHUNK + part * BLOCK)
            return carry

        if last - first == CHUNK:
            step(first // CHUNK, 0)
        else:
            lax.fori_loop(first // CHUNK, last // CHUNK, step, 0)

    def each_lane(body):
        def step(f, carry):
            body(f)
            return carry

        lax.fori_loop(0, lanes, step, 0)

    def unfold(from_ref, to_ref):
        def body(i, carry):
            f, part = i // 2, i % 2
            for t in range(lines // SUB):
                rows = from_ref[f, part, pl.ds(t * SUB, SUB), :]
                to_ref[f, part, pl.ds(t * SUB, SUB)] = rows.reshape(SUB, SUB, LANES)
            return carry

        lax.fori_loop(0, 2 * lanes, body, 0)

    def filter_y(y, taps, adjoint):
        return filtered(
            lambda o: tuple(padded[part, block(y + reach + o)] for part in range(3)),
            taps, adjoint,
        )

    def put_padded(y, re, im):
        padded[0, block(y + reach)] = re
        padded[1, block(y + reach)] = im
        padded[2, block(y + reach)] = re + im

    def slow_block(y):
        if whole_lines:
            return slow[block(y)]
        return slow[pl.ds(y * per_line, BLOCK * per_line)].reshape(BLOCK, SUB, LANES)

    def add_grad(y, term):
        if whole_lines:
            grad[block(y)] += term
        else:
            grad[pl.ds(y * per_line, BLOCK * per_line)] += term.reshape(
                BLOCK * per_line, SUB // per_line, LANES
            )

    def phases(f):
        w = angular(f)

        def body(y):
            s, co = sin_cos(w * slow_block(y))
            sine[f, block(y)] = s
            cosine[f, block(y)] = co

        each_block(0, lines, body)

    def forward(f, finish):
        taps = tap_list(f)

        def along_x(y):
            re, im = filter_x(wave[f, 0, block(y)], wave[f, 1, block(y)], taps, False)
            put_padded(y, re, im)

        def along_y(y):
            finish(f, y, *filter_y(y, taps, False))

        each_block(0, lines, along_x)
        each_block(0, lines, along_y)

    def turned(f, y, re, im):
        w, co, s = angular(f), cosine[f, block(y)], sine[f, block(y)]
        return w * (co * re - s * im), w * (s * re + co * im)

    def hop(f, chunk):
        rows = pl.ds(chunk * CHUNK, CHUNK)
        slot = f * chunks + chunk
        return pltpu.make_async_remote_copy(
            src_ref=leaving.at[f, rows], dst_ref=arrived.at[f, rows],
            send_sem=mu_send.at[slot], recv_sem=mu_recv.at[slot],
            device_id={"depth": lax.max(d - 1, 0)}, device_id_type=MESH,
        )

    def chain(f, use, taken):
        taps = tap_list(f)

        def take(chunk):
            @pl.when(d < depths - 1)
            def _():
                hop(f, chunk).wait_recv()

            def body(y):
                mu_re = adj[f, 0, block(y)] + arrived[f, block(y), 0]
                mu_im = adj[f, 1, block(y)] + arrived[f, block(y), 1]
                use(f, y, mu_re, mu_im)
                co, s = cosine[f, block(y)], sine[f, block(y)]
                put_padded(y, co * mu_re + s * mu_im, co * mu_im - s * mu_re)

            each_block(chunk * CHUNK, (chunk + 1) * CHUNK, body)

        def give(chunk):
            @pl.when(d > 0)
            def _():
                def body(y):
                    re, im = filter_y(y, taps, True)
                    re, im = filter_x(re, im, taps, True)
                    leaving[f, block(y), 0] = re
                    leaving[f, block(y), 1] = im

                each_block(chunk * CHUNK, (chunk + 1) * CHUNK, body)
                hop(f, chunk).start()

        for chunk in range(chunks):
            take(chunk)
            taken(f, chunk)
            if chunk > 0:
                give(chunk - 1)
        give(chunks - 1)

    def push_grad(to, sender):
        return pltpu.make_async_remote_copy(
            src_ref=grad.at[piece(to)], dst_ref=gathered.at[sender],
            send_sem=grad_send.at[to], recv_sem=grad_recv.at[sender],
            device_id={"freq": to}, device_id_type=MESH,
        )

    def send_grad(first, last):
        def step(to, carry):
            @pl.when(to != me)
            def _():
                push_grad(to, me).start()

            return carry

        lax.fori_loop(first, last, step, 0)

    early = d >= depths // 2

    @pl.when(early)
    def _():
        load_adjoint.wait()
        unfold(adjoint_in, adj)
        lax.fori_loop(1, peers, wait_slow, 0)

        def keep(f, y, mu_re, mu_im):
            adj[f, 0, block(y)] = mu_re
            adj[f, 1, block(y)] = mu_im

        def first(f):
            phases(f)
            chain(f, keep, lambda f, chunk: None)

        each_lane(first)
        load_source.wait()
        unfold(source_in, wave)

        def finish(f, y, re, im):
            re, im = turned(f, y, re, im)
            add_grad(y, adj[f, 1, block(y)] * re - adj[f, 0, block(y)] * im)

        each_lane(lambda f: forward(f, finish))
        send_grad(0, peers)

    @pl.when(jnp.logical_not(early))
    def _():
        load_source.wait()
        unfold(source_in, wave)

        def finish(f, y, re, im):
            wave[f, 0, block(y)] = re
            wave[f, 1, block(y)] = im

        each_lane(lambda f: forward(f, finish))
        load_adjoint.wait()
        unfold(adjoint_in, adj)
        lax.fori_loop(1, peers, wait_slow, 0)

        def turn(f):
            phases(f)

            def body(y):
                re, im = turned(f, y, wave[f, 0, block(y)], wave[f, 1, block(y)])
                wave[f, 0, block(y)] = re
                wave[f, 1, block(y)] = im

            each_block(0, lines, body)

        each_lane(turn)

        def use(f, y, mu_re, mu_im):
            add_grad(y, mu_im * wave[f, 0, block(y)] - mu_re * wave[f, 1, block(y)])

        def taken(f, chunk):
            @pl.when(f == lanes - 1)
            def _():
                done = [n * CHUNK * peers // lines for n in (chunk, chunk + 1)]
                send_grad(*done)

        each_lane(lambda f: chain(f, use, taken))

    gathered[me] = grad[piece(me)]

    def add(i, total):
        push_grad(me, peer(i)).wait_recv()
        return total + gathered[peer(i)]

    total = lax.fori_loop(1, peers, add, gathered[me])
    out_ref[...] = total * (1.0 / count)

    def drain(i, carry):
        push_slow(i, me).wait_send()
        push_grad(peer(i), me).wait_send()
        return carry

    lax.fori_loop(1, peers, drain, 0)

    @pl.when(d > 0)
    def _():
        def drain_mu(i, carry):
            hop(i // chunks, i % chunks).wait_send()
            return carry

        lax.fori_loop(0, lanes * chunks, drain_mu, 0)


def on_device(slowness, freq_index, taps, source_top, adjoint_source):
    lanes, _, _, lines, cells = source_top.shape
    peers, depths = lax.axis_size("freq"), lax.axis_size("depth")
    count, _, width = taps.shape
    reach = width // 2
    assert cells == SUB * LANES and slowness.shape[0] == 1
    rows = slowness.shape[1] // LANES
    whole_lines = rows % SUB == 0
    piece = (rows // SUB, SUB, LANES) if whole_lines else (1, rows, LANES)
    pieces = (piece[0] * peers,) + piece[1:]
    line = (SUB, LANES)
    f32 = jnp.float32
    vmem = pl.BlockSpec(memory_space=pltpu.VMEM)
    hbm = pl.BlockSpec(memory_space=pltpu.HBM)
    dma = pltpu.SemaphoreType.DMA
    chunks = lines // CHUNK
    out = pl.pallas_call(
        functools.partial(
            kernel, peers, depths, lanes, lines, reach, count, piece[0], whole_lines
        ),
        out_shape=jax.ShapeDtypeStruct(piece, f32),
        in_specs=[hbm] * 5,
        out_specs=vmem,
        scratch_shapes=[
            pltpu.VMEM(piece, f32),
            pltpu.SMEM((lanes,), jnp.int32),
            pltpu.SMEM((width, 2, count), f32),
            pltpu.VMEM((lanes, 2, lines, cells), f32),
            pltpu.VMEM((lanes, 2, lines, cells), f32),
            pltpu.VMEM((lanes, 2, lines) + line, f32),
            pltpu.VMEM((lanes, 2, lines) + line, f32),
            pltpu.VMEM((3, lines + 2 * reach) + line, f32),
            pltpu.VMEM(pieces, f32),
            pltpu.VMEM((lanes, lines) + line, f32),
            pltpu.VMEM((lanes, lines) + line, f32),
            pltpu.VMEM((lanes, lines, 2) + line, f32),
            pltpu.VMEM((lanes, lines, 2) + line, f32),
            pltpu.VMEM(pieces, f32),
            pltpu.VMEM((peers,) + piece, f32),
            dma((5,)),
            dma((peers,)),
            dma((peers,)),
            dma((lanes * chunks,)),
            dma((lanes * chunks,)),
            dma((peers,)),
            dma((peers,)),
        ],
        compiler_params=pltpu.CompilerParams(
            collective_id=0, has_side_effects=True, vmem_limit_bytes=56 * 1024 * 1024
        ),
    )(
        slowness.reshape(piece),
        freq_index,
        taps.transpose(2, 1, 0),
        source_top.reshape(lanes, 2, lines, cells),
        adjoint_source.reshape(lanes, 2, lines, cells),
    )
    return out.reshape(slowness.shape)


def solution(mesh):
    in_specs = (
        P("depth", "freq"),
        P("freq"),
        P(),
        P("freq", "depth", None, None, None),
        P("freq", "depth", None, None, None),
    )
    out_specs = P("depth", "freq")
    return jax.shard_map(
        on_device, mesh=mesh, in_specs=in_specs, out_specs=out_specs, check_vma=False
    )
```

```python
import functools
import math

import jax
import jax.numpy as jnp
from jax import lax
from jax.experimental import pallas as pl
from jax.experimental.pallas import tpu as pltpu
from jax.sharding import PartitionSpec as P

MESH = pl.DeviceIdType.MESH
LANES = 128
SUB = 8
BLOCK = 4
STEP = 8
CHUNK = 4

PI_HIGH = 3.140625
PI_LOW = math.pi - PI_HIGH


def sin_cos(phase):
    turns = jnp.floor(phase * (1.0 / math.pi) + 0.5)
    rest = (phase - turns * PI_HIGH) - turns * PI_LOW
    sign = 1.0 - 2.0 * (turns - 2.0 * jnp.floor(turns * 0.5))
    square = rest * rest
    odd = -1.0 / math.factorial(11)
    for n, s in ((9, 1), (7, -1), (5, 1), (3, -1), (1, 1)):
        odd = odd * square + s / math.factorial(n)
    even = 1.0 / math.factorial(12)
    for n, s in ((10, -1), (8, 1), (6, -1), (4, 1), (2, -1), (0, 1)):
        even = even * square + s / math.factorial(n)
    return sign * rest * odd, sign * even


def shifted(value, reach):
    lane = lax.broadcasted_iota(jnp.int32, value.shape, 2)
    row = lax.broadcasted_iota(jnp.int32, value.shape, 1)
    after = jnp.where(row < SUB - 1, pltpu.roll(value, SUB - 1, 1), 0.0)
    before = jnp.where(row > 0, pltpu.roll(value, 1, 1), 0.0)
    out = {0: value}
    for o in range(1, reach + 1):
        out[o] = pltpu.roll(jnp.where(lane >= o, value, after), LANES - o, 2)
        out[-o] = pltpu.roll(jnp.where(lane < LANES - o, value, before), o, 2)
    return out


def filtered(at, taps, adjoint):
    reach = len(taps) // 2
    total = None
    for k, (t_re, t_im) in enumerate(taps):
        o = reach - k if adjoint else k - reach
        u_re, u_im, u_sum = at(o)
        if adjoint:
            t_im = -t_im
        new = (t_re * u_sum, (t_im - t_re) * u_re, (t_re + t_im) * u_im)
        total = new if total is None else tuple(x + y for x, y in zip(total, new))
    a, b, c = total
    return a - c, a + b


def filter_x(re, im, taps, adjoint):
    reach = len(taps) // 2
    all_re, all_im = shifted(re, reach), shifted(im, reach)
    return filtered(lambda o: (all_re[o], all_im[o], all_re[o] + all_im[o]), taps, adjoint)


def kernel(
    peers, depths, lanes, lines, reach, count, per_piece, whole_lines,
    slow_hbm, index_hbm, taps_hbm, source_hbm, adjoint_hbm, out_ref,
    slow_ref, index_ref, taps_ref, source_in, adjoint_in, wave, adj, padded, slow, cosine, sine,
    arrived, leaving, grad, gathered,
    in_sem, slow_send, slow_recv, mu_send, mu_recv, grad_send, grad_recv,
):
    me = lax.axis_index("freq")
    d = lax.axis_index("depth")
    chunks = lines // CHUNK
    per_line = max(1, peers // lines)

    load_slow = pltpu.make_async_copy(slow_hbm, slow_ref, in_sem.at[0])
    load_index = pltpu.make_async_copy(index_hbm, index_ref, in_sem.at[1])
    load_taps = pltpu.make_async_copy(taps_hbm, taps_ref, in_sem.at[2])
    load_adjoint = pltpu.make_async_copy(adjoint_hbm, adjoint_in, in_sem.at[3])
    load_source = pltpu.make_async_copy(source_hbm, source_in, in_sem.at[4])

    barrier = pltpu.get_barrier_semaphore()

    def peer(i):
        return lax.rem(me + i, peers)

    def greet(i, carry):
        pl.semaphore_signal(barrier, inc=1, device_id={"freq": peer(i)}, device_id_type=MESH)
        return carry

    lax.fori_loop(1, peers, greet, 0)

    @pl.when(d < depths - 1)
    def _():
        pl.semaphore_signal(barrier, inc=1, device_id={"depth": d + 1}, device_id_type=MESH)

    for load in (load_slow, load_index, load_taps, load_adjoint, load_source):
        load.start()

    def piece(i):
        return pl.ds(i * per_piece, per_piece)

    margin = jnp.zeros((reach, SUB, LANES), jnp.float32)
    for part in range(3):
        padded[part, pl.ds(0, reach)] = margin
        padded[part, pl.ds(lines + reach, reach)] = margin
    grad[...] = jnp.zeros_like(grad)

    @pl.when(d == depths - 1)
    def _():
        arrived[...] = jnp.zeros_like(arrived)

    load_slow.wait()
    slow[piece(me)] = slow_ref[...]
    pl.semaphore_wait(barrier, jnp.where(d > 0, peers, peers - 1))

    def push_slow(i, sender):
        return pltpu.make_async_remote_copy(
            src_ref=slow_ref, dst_ref=slow.at[piece(sender)],
            send_sem=slow_send.at[peer(i)], recv_sem=slow_recv.at[sender],
            device_id={"freq": peer(i)}, device_id_type=MESH,
        )

    def start_slow(i, carry):
        push_slow(i, me).start()
        return carry

    lax.fori_loop(1, peers, start_slow, 0)
    load_index.wait()
    load_taps.wait()

    def wait_slow(i, carry):
        push_slow(i, peer(i)).wait_recv()
        return carry

    def tap_list(f):
        row = index_ref[f]
        return [(taps_ref[k, 0, row], taps_ref[k, 1, row]) for k in range(2 * reach + 1)]

    def angular(f):
        return 8.0 * (index_ref[f].astype(jnp.float32) + 1.0) / count

    def block(y):
        return pl.ds(y, BLOCK)

    def each_block(first, last, body):
        if last - first <= STEP:
            for y in range(first, last, BLOCK):
                body(y)
            return

        def step(b, carry):
            for part in range(STEP // BLOCK):
                body(b * STEP + part * BLOCK)
            return carry

        lax.fori_loop(first // STEP, last // STEP, step, 0)

    def each_lane(body):
        def step(f, carry):
            body(f)
            return carry

        lax.fori_loop(0, lanes, step, 0)

    def unfold(from_ref, to_ref):
        def body(i, carry):
            f, part = i // 2, i % 2
            for t in range(lines // SUB):
                rows = from_ref[f, part, pl.ds(t * SUB, SUB), :]
                to_ref[f, part, pl.ds(t * SUB, SUB)] = rows.reshape(SUB, SUB, LANES)
            return carry

        lax.fori_loop(0, 2 * lanes, body, 0)

    def filter_y(y, taps, adjoint):
        return filtered(
            lambda o: tuple(padded[part, block(y + reach + o)] for part in range(3)),
            taps, adjoint,
        )

    def put_padded(y, re, im):
        padded[0, block(y + reach)] = re
        padded[1, block(y + reach)] = im
        padded[2, block(y + reach)] = re + im

    def slow_block(y):
        if whole_lines:
            return slow[block(y)]
        return slow[pl.ds(y * per_line, BLOCK * per_line)].reshape(BLOCK, SUB, LANES)

    def add_grad(y, term):
        if whole_lines:
            grad[block(y)] += term
        else:
            grad[pl.ds(y * per_line, BLOCK * per_line)] += term.reshape(
                BLOCK * per_line, SUB // per_line, LANES
            )

    def phases(f, first=0, last=lines):
        w = angular(f)

        def body(y):
            s, co = sin_cos(w * slow_block(y))
            sine[f, block(y)] = s
            cosine[f, block(y)] = co

        each_block(first, last, body)

    def forward(f, finish):
        taps = tap_list(f)

        def along_x(y):
            re, im = filter_x(wave[f, 0, block(y)], wave[f, 1, block(y)], taps, False)
            put_padded(y, re, im)

        def along_y(y):
            finish(f, y, *filter_y(y, taps, False))

        each_block(0, lines, along_x)
        each_block(0, lines, along_y)

    def turned(f, y, re, im):
        w, co, s = angular(f), cosine[f, block(y)], sine[f, block(y)]
        return w * (co * re - s * im), w * (s * re + co * im)

    def hop(f, chunk):
        rows = pl.ds(chunk * CHUNK, CHUNK)
        slot = f * chunks + chunk
        return pltpu.make_async_remote_copy(
            src_ref=leaving.at[f, rows], dst_ref=arrived.at[f, rows],
            send_sem=mu_send.at[slot], recv_sem=mu_recv.at[slot],
            device_id={"depth": lax.max(d - 1, 0)}, device_id_type=MESH,
        )

    def chain(f, before, use, taken, x_first):
        taps = tap_list(f)
        lag = -(-reach // CHUNK)

        def take(chunk):
            @pl.when(d < depths - 1)
            def _():
                hop(f, chunk).wait_recv()

            before(f, chunk)
            first, last = chunk * CHUNK, (chunk + 1) * CHUNK

            def mu(y):
                return adj[f, 0, block(y)] + arrived[f, block(y), 0], adj[f, 1, block(y)] + arrived[f, block(y), 1]

            @pl.when(d > 0)
            def _():
                def body(y):
                    mu_re, mu_im = mu(y)
                    co, s = cosine[f, block(y)], sine[f, block(y)]
                    re, im = co * mu_re + s * mu_im, co * mu_im - s * mu_re
                    if x_first:
                        re, im = filter_x(re, im, taps, True)
                    put_padded(y, re, im)

                each_block(first, last, body)

            each_block(first, last, lambda y: use(f, y, *mu(y)))

        def give(chunk):
            @pl.when(d > 0)
            def _():
                def body(y):
                    re, im = filter_y(y, taps, True)
                    if not x_first:
                        re, im = filter_x(re, im, taps, True)
                    leaving[f, block(y), 0] = re
                    leaving[f, block(y), 1] = im

                each_block(chunk * CHUNK, (chunk + 1) * CHUNK, body)
                hop(f, chunk).start()

        for chunk in range(chunks):
            take(chunk)
            if chunk >= lag:
                give(chunk - lag)
            if chunk < chunks - 1:
                taken(f, chunk)
        for chunk in range(chunks - lag, chunks):
            give(chunk)
        taken(f, chunks - 1)

    def push_grad(to, sender):
        return pltpu.make_async_remote_copy(
            src_ref=grad.at[piece(to)], dst_ref=gathered.at[sender],
            send_sem=grad_send.at[to], recv_sem=grad_recv.at[sender],
            device_id={"freq": to}, device_id_type=MESH,
        )

    def send_grad(first, last):
        def step(to, carry):
            @pl.when(to != me)
            def _():
                push_grad(to, me).start()

            return carry

        lax.fori_loop(first, last, step, 0)

    early = d >= depths // 2

    @pl.when(early)
    def _():
        load_adjoint.wait()
        unfold(adjoint_in, adj)
        lax.fori_loop(1, peers, wait_slow, 0)

        def keep(f, y, mu_re, mu_im):
            adj[f, 0, block(y)] = mu_re
            adj[f, 1, block(y)] = mu_im

        @pl.when(d < depths - 1)
        def _():
            each_lane(phases)

        def before(f, chunk):
            @pl.when(d == depths - 1)
            def _():
                phases(f, chunk * CHUNK, (chunk + 1) * CHUNK)

        each_lane(lambda f: chain(f, before, keep, lambda f, chunk: None, False))
        load_source.wait()
        unfold(source_in, wave)

        def finish(f, y, re, im):
            re, im = turned(f, y, re, im)
            add_grad(y, adj[f, 1, block(y)] * re - adj[f, 0, block(y)] * im)

        each_lane(lambda f: forward(f, finish))
        send_grad(0, peers)

    @pl.when(jnp.logical_not(early))
    def _():
        load_source.wait()
        unfold(source_in, wave)

        def finish(f, y, re, im):
            wave[f, 0, block(y)] = re
            wave[f, 1, block(y)] = im

        each_lane(lambda f: forward(f, finish))
        load_adjoint.wait()
        unfold(adjoint_in, adj)
        lax.fori_loop(1, peers, wait_slow, 0)

        def turn(f):
            phases(f)

            def body(y):
                re, im = turned(f, y, wave[f, 0, block(y)], wave[f, 1, block(y)])
                wave[f, 0, block(y)] = re
                wave[f, 1, block(y)] = im

            each_block(0, lines, body)

        each_lane(turn)

        def use(f, y, mu_re, mu_im):
            add_grad(y, mu_im * wave[f, 0, block(y)] - mu_re * wave[f, 1, block(y)])

        def taken(f, chunk):
            @pl.when(f == lanes - 1)
            def _():
                done = [n * CHUNK * peers // lines for n in (chunk, chunk + 1)]
                send_grad(*done)

        each_lane(lambda f: chain(f, lambda f, chunk: None, use, taken, True))

    gathered[me] = grad[piece(me)]

    def add(i, total):
        push_grad(me, peer(i)).wait_recv()
        return total + gathered[peer(i)]

    total = lax.fori_loop(1, peers, add, gathered[me])
    out_ref[...] = total * (1.0 / count)

    def drain(i, carry):
        push_slow(i, me).wait_send()
        push_grad(peer(i), me).wait_send()
        return carry

    lax.fori_loop(1, peers, drain, 0)

    @pl.when(d > 0)
    def _():
        def drain_mu(i, carry):
            hop(i // chunks, i % chunks).wait_send()
            return carry

        lax.fori_loop(0, lanes * chunks, drain_mu, 0)


def on_device(slowness, freq_index, taps, source_top, adjoint_source):
    lanes, _, _, lines, cells = source_top.shape
    peers, depths = lax.axis_size("freq"), lax.axis_size("depth")
    count, _, width = taps.shape
    reach = width // 2
    assert cells == SUB * LANES and slowness.shape[0] == 1
    rows = slowness.shape[1] // LANES
    whole_lines = rows % SUB == 0
    piece = (rows // SUB, SUB, LANES) if whole_lines else (1, rows, LANES)
    pieces = (piece[0] * peers,) + piece[1:]
    line = (SUB, LANES)
    f32 = jnp.float32
    vmem = pl.BlockSpec(memory_space=pltpu.VMEM)
    hbm = pl.BlockSpec(memory_space=pltpu.HBM)
    dma = pltpu.SemaphoreType.DMA
    chunks = lines // CHUNK
    out = pl.pallas_call(
        functools.partial(
            kernel, peers, depths, lanes, lines, reach, count, piece[0], whole_lines
        ),
        out_shape=jax.ShapeDtypeStruct(piece, f32),
        in_specs=[hbm] * 5,
        out_specs=vmem,
        scratch_shapes=[
            pltpu.VMEM(piece, f32),
            pltpu.SMEM((lanes,), jnp.int32),
            pltpu.SMEM((width, 2, count), f32),
            pltpu.VMEM((lanes, 2, lines, cells), f32),
            pltpu.VMEM((lanes, 2, lines, cells), f32),
            pltpu.VMEM((lanes, 2, lines) + line, f32),
            pltpu.VMEM((lanes, 2, lines) + line, f32),
            pltpu.VMEM((3, lines + 2 * reach) + line, f32),
            pltpu.VMEM(pieces, f32),
            pltpu.VMEM((lanes, lines) + line, f32),
            pltpu.VMEM((lanes, lines) + line, f32),
            pltpu.VMEM((lanes, lines, 2) + line, f32),
            pltpu.VMEM((lanes, lines, 2) + line, f32),
            pltpu.VMEM(pieces, f32),
            pltpu.VMEM((peers,) + piece, f32),
            dma((5,)),
            dma((peers,)),
            dma((peers,)),
            dma((lanes * chunks,)),
            dma((lanes * chunks,)),
            dma((peers,)),
            dma((peers,)),
        ],
        compiler_params=pltpu.CompilerParams(
            collective_id=0, has_side_effects=True, vmem_limit_bytes=56 * 1024 * 1024
        ),
    )(
        slowness.reshape(piece),
        freq_index,
        taps.transpose(2, 1, 0),
        source_top.reshape(lanes, 2, lines, cells),
        adjoint_source.reshape(lanes, 2, lines, cells),
    )
    return out.reshape(slowness.shape)


def solution(mesh):
    in_specs = (
        P("depth", "freq"),
        P("freq"),
        P(),
        P("freq", "depth", None, None, None),
        P("freq", "depth", None, None, None),
    )
    out_specs = P("depth", "freq")
    return jax.shard_map(
        on_device, mesh=mesh, in_specs=in_specs, out_specs=out_specs, check_vma=False
    )
```

```python
import functools
import math

import jax
import jax.numpy as jnp
from jax import lax
from jax.experimental import pallas as pl
from jax.experimental.pallas import tpu as pltpu
from jax.sharding import PartitionSpec as P

MESH = pl.DeviceIdType.MESH
LANES = 128
SUB = 8
BLOCK = 4
STEP = 8
CHUNK = 4

PI_HIGH = 3.140625
PI_LOW = math.pi - PI_HIGH


def sin_cos(phase):
    turns = jnp.floor(phase * (1.0 / math.pi) + 0.5)
    rest = (phase - turns * PI_HIGH) - turns * PI_LOW
    sign = 1.0 - 2.0 * (turns - 2.0 * jnp.floor(turns * 0.5))
    square = rest * rest
    odd = -1.0 / math.factorial(11)
    for n, s in ((9, 1), (7, -1), (5, 1), (3, -1), (1, 1)):
        odd = odd * square + s / math.factorial(n)
    even = 1.0 / math.factorial(12)
    for n, s in ((10, -1), (8, 1), (6, -1), (4, 1), (2, -1), (0, 1)):
        even = even * square + s / math.factorial(n)
    return sign * rest * odd, sign * even


def shifted(value, reach):
    lane = lax.broadcasted_iota(jnp.int32, value.shape, 2)
    row = lax.broadcasted_iota(jnp.int32, value.shape, 1)
    after = jnp.where(row < SUB - 1, pltpu.roll(value, SUB - 1, 1), 0.0)
    before = jnp.where(row > 0, pltpu.roll(value, 1, 1), 0.0)
    out = {0: value}
    for o in range(1, reach + 1):
        out[o] = pltpu.roll(jnp.where(lane >= o, value, after), LANES - o, 2)
        out[-o] = pltpu.roll(jnp.where(lane < LANES - o, value, before), o, 2)
    return out


def filtered(at, taps, adjoint):
    reach = len(taps) // 2
    total = None
    for k, (t_re, t_im) in enumerate(taps):
        o = reach - k if adjoint else k - reach
        u_re, u_im, u_sum = at(o)
        if adjoint:
            t_im = -t_im
        new = (t_re * u_sum, (t_im - t_re) * u_re, (t_re + t_im) * u_im)
        total = new if total is None else tuple(x + y for x, y in zip(total, new))
    a, b, c = total
    return a - c, a + b


def filter_x(re, im, taps, adjoint):
    reach = len(taps) // 2
    all_re, all_im = shifted(re, reach), shifted(im, reach)
    return filtered(lambda o: (all_re[o], all_im[o], all_re[o] + all_im[o]), taps, adjoint)


def kernel(
    peers, depths, lines, reach, count, per_piece, whole_lines,
    slow_hbm, index_hbm, taps_hbm, source_hbm, adjoint_hbm, out_ref,
    slow_ref, index_ref, taps_ref, source_in, adjoint_in, wave, adj, padded, slow, cosine, sine,
    arrived, leaving, carried, grad, gathered,
    in_sem, pair_send, pair_recv, slow_send, slow_recv, mu_send, mu_recv, grad_send, grad_recv,
):
    d = lax.axis_index("depth")
    core = d % 2
    base = d - core
    members = 2 * peers
    me = lax.axis_index("freq") * 2 + core
    chunks = lines // CHUNK
    per_line = max(1, peers // lines)
    from_below = d < depths - 2
    to_above = d >= 2

    load_slow = pltpu.make_async_copy(slow_hbm, slow_ref, in_sem.at[0])
    load_index = pltpu.make_async_copy(index_hbm, index_ref, in_sem.at[1])
    load_taps = pltpu.make_async_copy(taps_hbm, taps_ref, in_sem.at[2])
    load_adjoint = pltpu.make_async_copy(adjoint_hbm.at[core], adjoint_in.at[core], in_sem.at[3])
    load_source = pltpu.make_async_copy(source_hbm.at[core], source_in.at[core], in_sem.at[4])

    barrier = pltpu.get_barrier_semaphore()

    def other(i):
        return lax.rem(me + i, members)

    def device(member):
        return {"freq": member // 2, "depth": base + member % 2}

    def greet(i, carry):
        pl.semaphore_signal(barrier, inc=1, device_id=device(other(i)), device_id_type=MESH)
        return carry

    lax.fori_loop(1, members, greet, 0)

    @pl.when(from_below)
    def _():
        pl.semaphore_signal(barrier, inc=1, device_id={"depth": d + 2}, device_id_type=MESH)

    for load in (load_slow, load_index, load_taps, load_adjoint, load_source):
        load.start()

    def piece(i):
        return pl.ds(i * per_piece, per_piece)

    margin = jnp.zeros((reach, SUB, LANES), jnp.float32)
    for section in range(2):
        for part in range(3):
            padded[section, part, pl.ds(0, reach)] = margin
            padded[section, part, pl.ds(lines + reach, reach)] = margin
    grad[...] = jnp.zeros_like(grad)

    @pl.when(jnp.logical_not(from_below))
    def _():
        arrived[...] = jnp.zeros_like(arrived)

    load_slow.wait()
    slow[core, piece(me // 2)] = slow_ref[...]
    pl.semaphore_wait(barrier, jnp.where(to_above, members, members - 1))

    def push_slow(i, sender):
        return pltpu.make_async_remote_copy(
            src_ref=slow_ref, dst_ref=slow.at[sender % 2, piece(sender // 2)],
            send_sem=slow_send.at[other(i)], recv_sem=slow_recv.at[sender],
            device_id=device(other(i)), device_id_type=MESH,
        )

    def start_slow(i, carry):
        push_slow(i, me).start()
        return carry

    def push_pair(n, from_ref, to_ref, section):
        return pltpu.make_async_remote_copy(
            src_ref=from_ref.at[1 - core], dst_ref=to_ref.at[section],
            send_sem=pair_send.at[n], recv_sem=pair_recv.at[n],
            device_id={"depth": base + 1 - core}, device_id_type=MESH,
        )

    lax.fori_loop(1, members, start_slow, 0)
    push_pair(0, adjoint_hbm, adjoint_in, core).start()
    push_pair(1, source_hbm, source_in, core).start()
    load_index.wait()
    load_taps.wait()

    def wait_slow(i, carry):
        push_slow(i, other(i)).wait_recv()
        return carry

    row = index_ref[core]
    taps = [(taps_ref[k, 0, row], taps_ref[k, 1, row]) for k in range(2 * reach + 1)]
    w = 8.0 * (row.astype(jnp.float32) + 1.0) / count

    def block(y):
        return pl.ds(y, BLOCK)

    def each_block(first, last, body):
        if last - first <= STEP:
            for y in range(first, last, BLOCK):
                body(y)
            return

        def step(b, carry):
            for part in range(STEP // BLOCK):
                body(b * STEP + part * BLOCK)
            return carry

        lax.fori_loop(first // STEP, last // STEP, step, 0)

    def each_section(body):
        def step(i, carry):
            body(1 - i)
            return carry

        lax.fori_loop(0, 2, step, 0)

    def unfold(from_ref, to_ref):
        def body(i, carry):
            section, part = 1 - i // 2, i % 2
            for t in range(lines // SUB):
                rows = from_ref[section, part, pl.ds(t * SUB, SUB), :]
                to_ref[section, part, pl.ds(t * SUB, SUB)] = rows.reshape(SUB, SUB, LANES)
            return carry

        lax.fori_loop(0, 4, body, 0)

    def take_adjoint():
        load_adjoint.wait()
        push_pair(0, adjoint_hbm, adjoint_in, 1 - core).wait_recv()
        unfold(adjoint_in, adj)

    def take_source():
        load_source.wait()
        push_pair(1, source_hbm, source_in, 1 - core).wait_recv()
        unfold(source_in, wave)

    def filter_y(section, y, adjoint):
        return filtered(
            lambda o: tuple(padded[section, part, block(y + reach + o)] for part in range(3)),
            taps, adjoint,
        )

    def put_padded(section, y, re, im):
        padded[section, 0, block(y + reach)] = re
        padded[section, 1, block(y + reach)] = im
        padded[section, 2, block(y + reach)] = re + im

    def slow_block(section, y):
        if whole_lines:
            return slow[section, block(y)]
        rows = slow[section, pl.ds(y * per_line, BLOCK * per_line)]
        return rows.reshape(BLOCK, SUB, LANES)

    def add_grad(section, y, term):
        if whole_lines:
            grad[section, block(y)] += term
        else:
            grad[section, pl.ds(y * per_line, BLOCK * per_line)] += term.reshape(
                BLOCK * per_line, SUB // per_line, LANES
            )

    def phases(section, first=0, last=lines):
        def body(y):
            s, co = sin_cos(w * slow_block(section, y))
            sine[section, block(y)] = s
            cosine[section, block(y)] = co

        each_block(first, last, body)

    def forward(section, finish):
        def along_x(y):
            re, im = wave[section, 0, block(y)], wave[section, 1, block(y)]
            put_padded(section, y, *filter_x(re, im, taps, False))

        def along_y(y):
            finish(section, y, *filter_y(section, y, False))

        each_block(0, lines, along_x)
        each_block(0, lines, along_y)

    def turned(section, y, re, im):
        co, s = cosine[section, block(y)], sine[section, block(y)]
        return w * (co * re - s * im), w * (s * re + co * im)

    def hop(chunk):
        rows = pl.ds(chunk * CHUNK, CHUNK)
        return pltpu.make_async_remote_copy(
            src_ref=leaving.at[rows], dst_ref=arrived.at[rows],
            send_sem=mu_send.at[chunk], recv_sem=mu_recv.at[chunk],
            device_id={"depth": lax.max(d - 2, 0)}, device_id_type=MESH,
        )

    def chain(before, use, taken, x_first):
        lag = -(-reach // CHUNK)

        def take(section, chunk):
            if section == 1:
                @pl.when(from_below)
                def _():
                    hop(chunk).wait_recv()

            before(section, chunk)
            first, last = chunk * CHUNK, (chunk + 1) * CHUNK
            incoming = arrived if section == 1 else carried

            def mu(y):
                return (
                    adj[section, 0, block(y)] + incoming[block(y), 0],
                    adj[section, 1, block(y)] + incoming[block(y), 1],
                )

            def body(y):
                mu_re, mu_im = mu(y)
                co, s = cosine[section, block(y)], sine[section, block(y)]
                re, im = co * mu_re + s * mu_im, co * mu_im - s * mu_re
                if x_first:
                    re, im = filter_x(re, im, taps, True)
                put_padded(section, y, re, im)

            if section == 1:
                each_block(first, last, body)
            else:
                pl.when(to_above)(lambda: each_block(first, last, body))
            each_block(first, last, lambda y: use(section, y, *mu(y)))

        def give(section, chunk):
            outgoing = carried if section == 1 else leaving

            def body(y):
                re, im = filter_y(section, y, True)
                if not x_first:
                    re, im = filter_x(re, im, taps, True)
                outgoing[block(y), 0] = re
                outgoing[block(y), 1] = im

            each_block(chunk * CHUNK, (chunk + 1) * CHUNK, body)
            if section == 0:
                hop(chunk).start()

        for turn in range(chunks + 2 * lag):
            if turn < chunks:
                take(1, turn)
            if lag <= turn < chunks + lag:
                give(1, turn - lag)
                take(0, turn - lag)
            if turn >= 2 * lag:
                pl.when(to_above)(functools.partial(give, 0, turn - 2 * lag))
            if turn < chunks:
                taken(1, turn)
            if lag <= turn < chunks + lag:
                taken(0, turn - lag)

    def push_grad(to, section, sender):
        return pltpu.make_async_remote_copy(
            src_ref=grad.at[section, piece(to)], dst_ref=gathered.at[sender],
            send_sem=grad_send.at[to * 2 + section], recv_sem=grad_recv.at[sender],
            device_id={"freq": to, "depth": base + section}, device_id_type=MESH,
        )

    def send_grad(section, first, last):
        def step(to, carry):
            @pl.when(to * 2 + section != me)
            def _():
                push_grad(to, section, me).start()

            return carry

        lax.fori_loop(first, last, step, 0)

    early = d >= depths // 2

    @pl.when(early)
    def _():
        take_adjoint()
        lax.fori_loop(1, members, wait_slow, 0)

        @pl.when(from_below)
        def _():
            each_section(phases)

        def before(section, chunk):
            @pl.when(jnp.logical_not(from_below))
            def _():
                phases(section, chunk * CHUNK, (chunk + 1) * CHUNK)

        def keep(section, y, mu_re, mu_im):
            adj[section, 0, block(y)] = mu_re
            adj[section, 1, block(y)] = mu_im

        chain(before, keep, lambda section, chunk: None, False)
        take_source()

        def finish(section, y, re, im):
            re, im = turned(section, y, re, im)
            mu_re, mu_im = adj[section, 0, block(y)], adj[section, 1, block(y)]
            add_grad(section, y, mu_im * re - mu_re * im)

        def last(section):
            forward(section, finish)
            send_grad(section, 0, peers)

        each_section(last)

    @pl.when(jnp.logical_not(early))
    def _():
        take_source()

        def finish(section, y, re, im):
            wave[section, 0, block(y)] = re
            wave[section, 1, block(y)] = im

        each_section(lambda section: forward(section, finish))
        take_adjoint()
        lax.fori_loop(1, members, wait_slow, 0)

        def turn(section):
            phases(section)

            def body(y):
                re, im = turned(section, y, wave[section, 0, block(y)], wave[section, 1, block(y)])
                wave[section, 0, block(y)] = re
                wave[section, 1, block(y)] = im

            each_block(0, lines, body)

        each_section(turn)

        def use(section, y, mu_re, mu_im):
            re, im = wave[section, 0, block(y)], wave[section, 1, block(y)]
            add_grad(section, y, mu_im * re - mu_re * im)

        def taken(section, chunk):
            done = [n * CHUNK * peers // lines for n in (chunk, chunk + 1)]
            send_grad(section, *done)

        chain(lambda section, chunk: None, use, taken, True)

    gathered[me] = grad[core, piece(me // 2)]

    def add(i, total):
        push_grad(me // 2, core, other(i)).wait_recv()
        return total + gathered[other(i)]

    total = lax.fori_loop(1, members, add, gathered[me])
    out_ref[...] = total * (1.0 / count)

    def drain(i, carry):
        push_slow(i, me).wait_send()
        push_grad(other(i) // 2, other(i) % 2, me).wait_send()
        return carry

    lax.fori_loop(1, members, drain, 0)
    push_pair(0, adjoint_hbm, adjoint_in, core).wait_send()
    push_pair(1, source_hbm, source_in, core).wait_send()

    @pl.when(to_above)
    def _():
        def drain_mu(chunk, carry):
            hop(chunk).wait_send()
            return carry

        lax.fori_loop(0, chunks, drain_mu, 0)


def on_device(slowness, freq_index, taps, source_top, adjoint_source):
    lanes, _, _, lines, cells = source_top.shape
    peers, depths = lax.axis_size("freq"), lax.axis_size("depth")
    count, _, width = taps.shape
    reach = width // 2
    assert lanes == 2 and depths % 2 == 0 and cells == SUB * LANES and slowness.shape[0] == 1
    rows = slowness.shape[1] // LANES
    whole_lines = rows % SUB == 0
    piece = (rows // SUB, SUB, LANES) if whole_lines else (1, rows, LANES)
    pieces = (piece[0] * peers,) + piece[1:]
    line = (SUB, LANES)
    f32 = jnp.float32
    vmem = pl.BlockSpec(memory_space=pltpu.VMEM)
    hbm = pl.BlockSpec(memory_space=pltpu.HBM)
    dma = pltpu.SemaphoreType.DMA
    chunks = lines // CHUNK
    out = pl.pallas_call(
        functools.partial(
            kernel, peers, depths, lines, reach, count, piece[0], whole_lines
        ),
        out_shape=jax.ShapeDtypeStruct(piece, f32),
        in_specs=[hbm] * 5,
        out_specs=vmem,
        scratch_shapes=[
            pltpu.VMEM(piece, f32),
            pltpu.SMEM((lanes,), jnp.int32),
            pltpu.SMEM((width, 2, count), f32),
            pltpu.VMEM((2, 2, lines, cells), f32),
            pltpu.VMEM((2, 2, lines, cells), f32),
            pltpu.VMEM((2, 2, lines) + line, f32),
            pltpu.VMEM((2, 2, lines) + line, f32),
            pltpu.VMEM((2, 3, lines + 2 * reach) + line, f32),
            pltpu.VMEM((2,) + pieces, f32),
            pltpu.VMEM((2, lines) + line, f32),
            pltpu.VMEM((2, lines) + line, f32),
            pltpu.VMEM((lines, 2) + line, f32),
            pltpu.VMEM((lines, 2) + line, f32),
            pltpu.VMEM((lines, 2) + line, f32),
            pltpu.VMEM((2,) + pieces, f32),
            pltpu.VMEM((2 * peers,) + piece, f32),
            dma((5,)),
            dma((2,)),
            dma((2,)),
            dma((2 * peers,)),
            dma((2 * peers,)),
            dma((chunks,)),
            dma((chunks,)),
            dma((2 * peers,)),
            dma((2 * peers,)),
        ],
        compiler_params=pltpu.CompilerParams(
            collective_id=0, has_side_effects=True, vmem_limit_bytes=56 * 1024 * 1024
        ),
    )(
        slowness.reshape(piece),
        freq_index,
        taps.transpose(2, 1, 0),
        source_top.reshape(lanes, 2, lines, cells),
        adjoint_source.reshape(lanes, 2, lines, cells),
    )
    return out.reshape(slowness.shape)


def solution(mesh):
    in_specs = (
        P("depth", "freq"),
        P("freq"),
        P(),
        P("freq", "depth", None, None, None),
        P("freq", "depth", None, None, None),
    )
    out_specs = P("depth", "freq")
    return jax.shard_map(
        on_device, mesh=mesh, in_specs=in_specs, out_specs=out_specs, check_vma=False
    )
```

```python
import functools
import math

import jax
import jax.numpy as jnp
from jax import lax
from jax.experimental import pallas as pl
from jax.experimental.pallas import tpu as pltpu
from jax.sharding import PartitionSpec as P

MESH = pl.DeviceIdType.MESH
LANES = 128
SUB = 8
BLOCK = 4
STEP = 8
CHUNK = 8

PI_HIGH = 3.140625
PI_LOW = math.pi - PI_HIGH


def sin_cos(phase):
    turns = jnp.floor(phase * (1.0 / math.pi) + 0.5)
    rest = (phase - turns * PI_HIGH) - turns * PI_LOW
    sign = 1.0 - 2.0 * (turns - 2.0 * jnp.floor(turns * 0.5))
    square = rest * rest
    odd = -1.0 / math.factorial(11)
    for n, s in ((9, 1), (7, -1), (5, 1), (3, -1), (1, 1)):
        odd = odd * square + s / math.factorial(n)
    even = 1.0 / math.factorial(12)
    for n, s in ((10, -1), (8, 1), (6, -1), (4, 1), (2, -1), (0, 1)):
        even = even * square + s / math.factorial(n)
    return sign * rest * odd, sign * even


def shifted(value, reach):
    lane = lax.broadcasted_iota(jnp.int32, value.shape, 2)
    row = lax.broadcasted_iota(jnp.int32, value.shape, 1)
    after = jnp.where(row < SUB - 1, pltpu.roll(value, SUB - 1, 1), 0.0)
    before = jnp.where(row > 0, pltpu.roll(value, 1, 1), 0.0)
    out = {0: value}
    for o in range(1, reach + 1):
        out[o] = pltpu.roll(jnp.where(lane >= o, value, after), LANES - o, 2)
        out[-o] = pltpu.roll(jnp.where(lane < LANES - o, value, before), o, 2)
    return out


def filtered(at, taps, adjoint):
    reach = len(taps) // 2
    total = None
    for k, (t_re, t_im) in enumerate(taps):
        o = reach - k if adjoint else k - reach
        u_re, u_im, u_sum = at(o)
        if adjoint:
            t_im = -t_im
        new = (t_re * u_sum, (t_im - t_re) * u_re, (t_re + t_im) * u_im)
        total = new if total is None else tuple(x + y for x, y in zip(total, new))
    a, b, c = total
    return a - c, a + b


def filter_x(re, im, taps, adjoint):
    reach = len(taps) // 2
    all_re, all_im = shifted(re, reach), shifted(im, reach)
    return filtered(lambda o: (all_re[o], all_im[o], all_re[o] + all_im[o]), taps, adjoint)


def kernel(
    peers, depths, lanes, lines, reach, count, per_piece, whole_lines,
    slow_hbm, index_hbm, taps_hbm, source_hbm, adjoint_hbm, out_ref,
    slow_ref, index_ref, taps_ref, source_in, adjoint_in, wave, adj, padded, slow, cosine, sine,
    arrived, leaving, grad, gathered,
    in_sem, slow_send, slow_recv, mu_send, mu_recv, grad_send, grad_recv,
):
    me = lax.axis_index("freq")
    d = lax.axis_index("depth")
    chunks = lines // CHUNK
    per_line = max(1, peers // lines)

    load_slow = pltpu.make_async_copy(slow_hbm, slow_ref, in_sem.at[0])
    load_index = pltpu.make_async_copy(index_hbm, index_ref, in_sem.at[1])
    load_taps = pltpu.make_async_copy(taps_hbm, taps_ref, in_sem.at[2])
    load_adjoint = pltpu.make_async_copy(adjoint_hbm, adjoint_in, in_sem.at[3])
    load_source = pltpu.make_async_copy(source_hbm, source_in, in_sem.at[4])

    barrier = pltpu.get_barrier_semaphore()

    def peer(i):
        return lax.rem(me + i, peers)

    def greet(i, carry):
        pl.semaphore_signal(barrier, inc=1, device_id={"freq": peer(i)}, device_id_type=MESH)
        return carry

    lax.fori_loop(1, peers, greet, 0)

    @pl.when(d < depths - 1)
    def _():
        pl.semaphore_signal(barrier, inc=1, device_id={"depth": d + 1}, device_id_type=MESH)

    for load in (load_slow, load_index, load_taps, load_adjoint, load_source):
        load.start()

    def piece(i):
        return pl.ds(i * per_piece, per_piece)

    margin = jnp.zeros((reach, SUB, LANES), jnp.float32)
    for part in range(3):
        padded[part, pl.ds(0, reach)] = margin
        padded[part, pl.ds(lines + reach, reach)] = margin
    grad[...] = jnp.zeros_like(grad)

    @pl.when(d == depths - 1)
    def _():
        arrived[...] = jnp.zeros_like(arrived)

    load_slow.wait()
    slow[piece(me)] = slow_ref[...]
    pl.semaphore_wait(barrier, jnp.where(d > 0, peers, peers - 1))

    def push_slow(i, sender):
        return pltpu.make_async_remote_copy(
            src_ref=slow_ref, dst_ref=slow.at[piece(sender)],
            send_sem=slow_send.at[peer(i)], recv_sem=slow_recv.at[sender],
            device_id={"freq": peer(i)}, device_id_type=MESH,
        )

    def start_slow(i, carry):
        push_slow(i, me).start()
        return carry

    lax.fori_loop(1, peers, start_slow, 0)
    load_index.wait()
    load_taps.wait()

    def wait_slow(i, carry):
        push_slow(i, peer(i)).wait_recv()
        return carry

    def drain_slow(i, carry):
        push_slow(i, me).wait_send()
        return carry

    def tap_list(f):
        row = index_ref[f]
        return [(taps_ref[k, 0, row], taps_ref[k, 1, row]) for k in range(2 * reach + 1)]

    def angular(f):
        return 8.0 * (index_ref[f].astype(jnp.float32) + 1.0) / count

    def block(y):
        return pl.ds(y, BLOCK)

    def each_block(first, last, body):
        if last - first <= STEP:
            for y in range(first, last, BLOCK):
                body(y)
            return

        def step(b, carry):
            for part in range(STEP // BLOCK):
                body(b * STEP + part * BLOCK)
            return carry

        lax.fori_loop(first // STEP, last // STEP, step, 0)

    def each_lane(body):
        def step(f, carry):
            body(f)
            return carry

        lax.fori_loop(0, lanes, step, 0)

    def unfold(from_ref, to_ref):
        def body(i, carry):
            f, part = i // 2, i % 2
            for t in range(lines // SUB):
                rows = from_ref[f, part, pl.ds(t * SUB, SUB), :]
                to_ref[f, part, pl.ds(t * SUB, SUB)] = rows.reshape(SUB, SUB, LANES)
            return carry

        lax.fori_loop(0, 2 * lanes, body, 0)

    def filter_y(y, taps, adjoint):
        return filtered(
            lambda o: tuple(padded[part, block(y + reach + o)] for part in range(3)),
            taps, adjoint,
        )

    def put_padded(y, re, im):
        padded[0, block(y + reach)] = re
        padded[1, block(y + reach)] = im
        padded[2, block(y + reach)] = re + im

    def slow_block(y):
        if whole_lines:
            return slow[block(y)]
        return slow[pl.ds(y * per_line, BLOCK * per_line)].reshape(BLOCK, SUB, LANES)

    def add_grad(y, term):
        if whole_lines:
            grad[block(y)] += term
        else:
            grad[pl.ds(y * per_line, BLOCK * per_line)] += term.reshape(
                BLOCK * per_line, SUB // per_line, LANES
            )

    def phases(f, first=0, last=lines):
        w = angular(f)

        def body(y):
            s, co = sin_cos(w * slow_block(y))
            sine[f, block(y)] = s
            cosine[f, block(y)] = co

        each_block(first, last, body)

    def forward(f, finish):
        taps = tap_list(f)

        def along_x(y):
            re, im = filter_x(wave[f, 0, block(y)], wave[f, 1, block(y)], taps, False)
            put_padded(y, re, im)

        def along_y(y):
            finish(f, y, *filter_y(y, taps, False))

        each_block(0, lines, along_x)
        each_block(0, lines, along_y)

    def turned(f, y, re, im):
        w, co, s = angular(f), cosine[f, block(y)], sine[f, block(y)]
        return w * (co * re - s * im), w * (s * re + co * im)

    def hop(f, chunk):
        rows = pl.ds(chunk * CHUNK, CHUNK)
        slot = f * chunks + chunk
        return pltpu.make_async_remote_copy(
            src_ref=leaving.at[f, rows], dst_ref=arrived.at[f, rows],
            send_sem=mu_send.at[slot], recv_sem=mu_recv.at[slot],
            device_id={"depth": lax.max(d - 1, 0)}, device_id_type=MESH,
        )

    def chain(f, before, use, taken, x_first):
        taps = tap_list(f)
        lag = -(-reach // CHUNK)

        def take(chunk):
            @pl.when(d < depths - 1)
            def _():
                hop(f, chunk).wait_recv()

            before(f, chunk)
            first, last = chunk * CHUNK, (chunk + 1) * CHUNK

            def mu(y):
                return adj[f, 0, block(y)] + arrived[f, block(y), 0], adj[f, 1, block(y)] + arrived[f, block(y), 1]

            @pl.when(d > 0)
            def _():
                def body(y):
                    mu_re, mu_im = mu(y)
                    co, s = cosine[f, block(y)], sine[f, block(y)]
                    re, im = co * mu_re + s * mu_im, co * mu_im - s * mu_re
                    if x_first:
                        re, im = filter_x(re, im, taps, True)
                    put_padded(y, re, im)

                each_block(first, last, body)

            each_block(first, last, lambda y: use(f, y, *mu(y)))

        def give(chunk):
            @pl.when(d > 0)
            def _():
                def body(y):
                    re, im = filter_y(y, taps, True)
                    if not x_first:
                        re, im = filter_x(re, im, taps, True)
                    leaving[f, block(y), 0] = re
                    leaving[f, block(y), 1] = im

                each_block(chunk * CHUNK, (chunk + 1) * CHUNK, body)
                hop(f, chunk).start()

        for chunk in range(chunks):
            take(chunk)
            if chunk >= lag:
                give(chunk - lag)
            if chunk < chunks - 1:
                taken(f, chunk)
        for chunk in range(chunks - lag, chunks):
            give(chunk)
        taken(f, chunks - 1)

    def push_grad(to, sender):
        return pltpu.make_async_remote_copy(
            src_ref=grad.at[piece(to)], dst_ref=gathered.at[sender],
            send_sem=grad_send.at[to], recv_sem=grad_recv.at[sender],
            device_id={"freq": to}, device_id_type=MESH,
        )

    def send_grad(first, last):
        def step(to, carry):
            @pl.when(to != me)
            def _():
                push_grad(to, me).start()

            return carry

        lax.fori_loop(first, last, step, 0)

    early = d >= depths // 2

    @pl.when(early)
    def _():
        load_adjoint.wait()
        unfold(adjoint_in, adj)
        lax.fori_loop(1, peers, wait_slow, 0)

        def keep(f, y, mu_re, mu_im):
            adj[f, 0, block(y)] = mu_re
            adj[f, 1, block(y)] = mu_im

        @pl.when(d < depths - 1)
        def _():
            each_lane(phases)

        def before(f, chunk):
            @pl.when(d == depths - 1)
            def _():
                phases(f, chunk * CHUNK, (chunk + 1) * CHUNK)

        each_lane(lambda f: chain(f, before, keep, lambda f, chunk: None, False))
        lax.fori_loop(1, peers, drain_slow, 0)
        load_source.wait()
        unfold(source_in, wave)

        def finish(f, y, re, im):
            re, im = turned(f, y, re, im)
            add_grad(y, adj[f, 1, block(y)] * re - adj[f, 0, block(y)] * im)

        each_lane(lambda f: forward(f, finish))
        send_grad(0, peers)

    @pl.when(jnp.logical_not(early))
    def _():
        load_source.wait()
        unfold(source_in, wave)

        def finish(f, y, re, im):
            wave[f, 0, block(y)] = re
            wave[f, 1, block(y)] = im

        each_lane(lambda f: forward(f, finish))
        load_adjoint.wait()
        unfold(adjoint_in, adj)
        lax.fori_loop(1, peers, wait_slow, 0)

        def turn(f):
            phases(f)

            def body(y):
                re, im = turned(f, y, wave[f, 0, block(y)], wave[f, 1, block(y)])
                wave[f, 0, block(y)] = re
                wave[f, 1, block(y)] = im

            each_block(0, lines, body)

        each_lane(turn)
        lax.fori_loop(1, peers, drain_slow, 0)

        def use(f, y, mu_re, mu_im):
            add_grad(y, mu_im * wave[f, 0, block(y)] - mu_re * wave[f, 1, block(y)])

        def taken(f, chunk):
            @pl.when(f == lanes - 1)
            def _():
                done = [n * CHUNK * peers // lines for n in (chunk, chunk + 1)]
                send_grad(*done)

        each_lane(lambda f: chain(f, lambda f, chunk: None, use, taken, True))

    gathered[me] = grad[piece(me)]

    def add(i, total):
        push_grad(me, peer(i)).wait_recv()
        return total + gathered[peer(i)]

    total = lax.fori_loop(1, peers, add, gathered[me])
    out_ref[...] = total * (1.0 / count)

    def drain(i, carry):
        push_grad(peer(i), me).wait_send()
        return carry

    lax.fori_loop(1, peers, drain, 0)

    @pl.when(d > 0)
    def _():
        def drain_mu(i, carry):
            hop(i // chunks, i % chunks).wait_send()
            return carry

        lax.fori_loop(0, lanes * chunks, drain_mu, 0)


def on_device(slowness, freq_index, taps, source_top, adjoint_source):
    lanes, _, _, lines, cells = source_top.shape
    peers, depths = lax.axis_size("freq"), lax.axis_size("depth")
    count, _, width = taps.shape
    reach = width // 2
    assert cells == SUB * LANES and slowness.shape[0] == 1
    rows = slowness.shape[1] // LANES
    whole_lines = rows % SUB == 0
    piece = (rows // SUB, SUB, LANES) if whole_lines else (1, rows, LANES)
    pieces = (piece[0] * peers,) + piece[1:]
    line = (SUB, LANES)
    f32 = jnp.float32
    vmem = pl.BlockSpec(memory_space=pltpu.VMEM)
    hbm = pl.BlockSpec(memory_space=pltpu.HBM)
    dma = pltpu.SemaphoreType.DMA
    chunks = lines // CHUNK
    out = pl.pallas_call(
        functools.partial(
            kernel, peers, depths, lanes, lines, reach, count, piece[0], whole_lines
        ),
        out_shape=jax.ShapeDtypeStruct(piece, f32),
        in_specs=[hbm] * 5,
        out_specs=vmem,
        scratch_shapes=[
            pltpu.VMEM(piece, f32),
            pltpu.SMEM((lanes,), jnp.int32),
            pltpu.SMEM((width, 2, count), f32),
            pltpu.VMEM((lanes, 2, lines, cells), f32),
            pltpu.VMEM((lanes, 2, lines, cells), f32),
            pltpu.VMEM((lanes, 2, lines) + line, f32),
            pltpu.VMEM((lanes, 2, lines) + line, f32),
            pltpu.VMEM((3, lines + 2 * reach) + line, f32),
            pltpu.VMEM(pieces, f32),
            pltpu.VMEM((lanes, lines) + line, f32),
            pltpu.VMEM((lanes, lines) + line, f32),
            pltpu.VMEM((lanes, lines, 2) + line, f32),
            pltpu.VMEM((lanes, lines, 2) + line, f32),
            pltpu.VMEM(pieces, f32),
            pltpu.VMEM((peers,) + piece, f32),
            dma((5,)),
            dma((peers,)),
            dma((peers,)),
            dma((lanes * chunks,)),
            dma((lanes * chunks,)),
            dma((peers,)),
            dma((peers,)),
        ],
        compiler_params=pltpu.CompilerParams(
            collective_id=0, has_side_effects=True, vmem_limit_bytes=56 * 1024 * 1024
        ),
    )(
        slowness.reshape(piece),
        freq_index,
        taps.transpose(2, 1, 0),
        source_top.reshape(lanes, 2, lines, cells),
        adjoint_source.reshape(lanes, 2, lines, cells),
    )
    return out.reshape(slowness.shape)


def solution(mesh):
    in_specs = (
        P("depth", "freq"),
        P("freq"),
        P(),
        P("freq", "depth", None, None, None),
        P("freq", "depth", None, None, None),
    )
    out_specs = P("depth", "freq")
    return jax.shard_map(
        on_device, mesh=mesh, in_specs=in_specs, out_specs=out_specs, check_vma=False
    )
```

```python
import functools
import math

import jax
import jax.numpy as jnp
from jax import lax
from jax.experimental import pallas as pl
from jax.experimental.pallas import tpu as pltpu
from jax.sharding import PartitionSpec as P

MESH = pl.DeviceIdType.MESH
LANES = 128
SUB = 8
BLOCK = 4
STEP = 8
CHUNK = 4

PI_HIGH = 3.140625
PI_LOW = math.pi - PI_HIGH


def sin_cos(phase):
    turns = jnp.floor(phase * (1.0 / math.pi) + 0.5)
    rest = (phase - turns * PI_HIGH) - turns * PI_LOW
    sign = 1.0 - 2.0 * (turns - 2.0 * jnp.floor(turns * 0.5))
    square = rest * rest
    odd = -1.0 / math.factorial(11)
    for n, s in ((9, 1), (7, -1), (5, 1), (3, -1), (1, 1)):
        odd = odd * square + s / math.factorial(n)
    even = 1.0 / math.factorial(12)
    for n, s in ((10, -1), (8, 1), (6, -1), (4, 1), (2, -1), (0, 1)):
        even = even * square + s / math.factorial(n)
    return sign * rest * odd, sign * even


def shifted(value, reach):
    lane = lax.broadcasted_iota(jnp.int32, value.shape, 2)
    row = lax.broadcasted_iota(jnp.int32, value.shape, 1)
    after = jnp.where(row < SUB - 1, pltpu.roll(value, SUB - 1, 1), 0.0)
    before = jnp.where(row > 0, pltpu.roll(value, 1, 1), 0.0)
    out = {0: value}
    for o in range(1, reach + 1):
        out[o] = pltpu.roll(jnp.where(lane >= o, value, after), LANES - o, 2)
        out[-o] = pltpu.roll(jnp.where(lane < LANES - o, value, before), o, 2)
    return out


def filtered(at, taps, adjoint):
    reach = len(taps) // 2
    total = None
    for k, (t_re, t_im) in enumerate(taps):
        o = reach - k if adjoint else k - reach
        u_re, u_im, u_sum = at(o)
        if adjoint:
            t_im = -t_im
        new = (t_re * u_sum, (t_im - t_re) * u_re, (t_re + t_im) * u_im)
        total = new if total is None else tuple(x + y for x, y in zip(total, new))
    a, b, c = total
    return a - c, a + b


def filter_x(re, im, taps, adjoint):
    reach = len(taps) // 2
    all_re, all_im = shifted(re, reach), shifted(im, reach)
    return filtered(lambda o: (all_re[o], all_im[o], all_re[o] + all_im[o]), taps, adjoint)


def kernel(
    peers, depths, lanes, lines, reach, count, per_piece, whole_lines,
    slow_hbm, index_hbm, taps_hbm, source_hbm, adjoint_hbm, out_ref,
    slow_ref, index_ref, taps_ref, source_in, adjoint_in, wave, adj, padded, slow, cosine, sine,
    arrived, leaving, grad, gathered,
    in_sem, slow_send, slow_recv, mu_send, mu_recv, grad_send, grad_recv,
):
    me = lax.axis_index("freq")
    d = lax.axis_index("depth")
    chunks = lines // CHUNK
    per_line = max(1, peers // lines)

    load_slow = pltpu.make_async_copy(slow_hbm, slow_ref, in_sem.at[0])
    load_index = pltpu.make_async_copy(index_hbm, index_ref, in_sem.at[1])
    load_taps = pltpu.make_async_copy(taps_hbm, taps_ref, in_sem.at[2])
    load_adjoint = pltpu.make_async_copy(adjoint_hbm, adjoint_in, in_sem.at[3])
    load_source = pltpu.make_async_copy(source_hbm, source_in, in_sem.at[4])

    barrier = pltpu.get_barrier_semaphore()

    def peer(i):
        return lax.rem(me + i, peers)

    def greet(i, carry):
        pl.semaphore_signal(barrier, inc=1, device_id={"freq": peer(i)}, device_id_type=MESH)
        return carry

    lax.fori_loop(1, peers, greet, 0)

    @pl.when(d < depths - 1)
    def _():
        pl.semaphore_signal(barrier, inc=1, device_id={"depth": d + 1}, device_id_type=MESH)

    for load in (load_slow, load_index, load_taps, load_adjoint, load_source):
        load.start()

    def piece(i):
        return pl.ds(i * per_piece, per_piece)

    margin = jnp.zeros((reach, SUB, LANES), jnp.float32)
    for part in range(3):
        padded[part, pl.ds(0, reach)] = margin
        padded[part, pl.ds(lines + reach, reach)] = margin
    grad[...] = jnp.zeros_like(grad)

    @pl.when(d == depths - 1)
    def _():
        arrived[...] = jnp.zeros_like(arrived)

    load_slow.wait()
    slow[piece(me)] = slow_ref[...]
    pl.semaphore_wait(barrier, jnp.where(d > 0, peers, peers - 1))

    def push_slow(i, sender):
        return pltpu.make_async_remote_copy(
            src_ref=slow_ref, dst_ref=slow.at[piece(sender)],
            send_sem=slow_send.at[peer(i)], recv_sem=slow_recv.at[sender],
            device_id={"freq": peer(i)}, device_id_type=MESH,
        )

    def start_slow(i, carry):
        push_slow(i, me).start()
        return carry

    lax.fori_loop(1, peers, start_slow, 0)
    load_index.wait()
    load_taps.wait()

    def wait_slow(i, carry):
        push_slow(i, peer(i)).wait_recv()
        return carry

    def drain_slow(i, carry):
        push_slow(i, me).wait_send()
        return carry

    def tap_list(f):
        row = index_ref[f]
        return [(taps_ref[k, 0, row], taps_ref[k, 1, row]) for k in range(2 * reach + 1)]

    def angular(f):
        return 8.0 * (index_ref[f].astype(jnp.float32) + 1.0) / count

    def block(y):
        return pl.ds(y, BLOCK)

    def each_block(first, last, body):
        if last - first <= STEP:
            for y in range(first, last, BLOCK):
                body(y)
            return

        def step(b, carry):
            for part in range(STEP // BLOCK):
                body(b * STEP + part * BLOCK)
            return carry

        lax.fori_loop(first // STEP, last // STEP, step, 0)

    def each_lane(body):
        def step(f, carry):
            body(f)
            return carry

        lax.fori_loop(0, lanes, step, 0)

    def unfold(from_ref, to_ref):
        def body(i, carry):
            f, part = i // 2, i % 2
            for t in range(lines // SUB):
                rows = from_ref[f, part, pl.ds(t * SUB, SUB), :]
                to_ref[f, part, pl.ds(t * SUB, SUB)] = rows.reshape(SUB, SUB, LANES)
            return carry

        lax.fori_loop(0, 2 * lanes, body, 0)

    def filter_y(y, taps, adjoint):
        return filtered(
            lambda o: tuple(padded[part, block(y + reach + o)] for part in range(3)),
            taps, adjoint,
        )

    def put_padded(y, re, im):
        padded[0, block(y + reach)] = re
        padded[1, block(y + reach)] = im
        padded[2, block(y + reach)] = re + im

    def slow_block(y):
        if whole_lines:
            return slow[block(y)]
        return slow[pl.ds(y * per_line, BLOCK * per_line)].reshape(BLOCK, SUB, LANES)

    def add_grad(y, term):
        if whole_lines:
            grad[block(y)] += term
        else:
            grad[pl.ds(y * per_line, BLOCK * per_line)] += term.reshape(
                BLOCK * per_line, SUB // per_line, LANES
            )

    def phases(f, first=0, last=lines):
        w = angular(f)

        def body(y):
            s, co = sin_cos(w * slow_block(y))
            sine[f, block(y)] = s
            cosine[f, block(y)] = co

        each_block(first, last, body)

    def forward(f, finish):
        taps = tap_list(f)

        def along_x(y):
            re, im = filter_x(wave[f, 0, block(y)], wave[f, 1, block(y)], taps, False)
            put_padded(y, re, im)

        def along_y(y):
            finish(f, y, *filter_y(y, taps, False))

        each_block(0, lines, along_x)
        each_block(0, lines, along_y)

    def turned(f, y, re, im):
        w, co, s = angular(f), cosine[f, block(y)], sine[f, block(y)]
        return w * (co * re - s * im), w * (s * re + co * im)

    def hop(f, chunk):
        rows = pl.ds(chunk * CHUNK, CHUNK)
        slot = f * chunks + chunk
        return pltpu.make_async_remote_copy(
            src_ref=leaving.at[f, rows], dst_ref=arrived.at[f, rows],
            send_sem=mu_send.at[slot], recv_sem=mu_recv.at[slot],
            device_id={"depth": lax.max(d - 1, 0)}, device_id_type=MESH,
        )

    def chain(f, before, use, taken):
        taps = tap_list(f)
        lag = -(-reach // CHUNK)

        def mu(y):
            return adj[f, 0, block(y)] + arrived[f, block(y), 0], adj[f, 1, block(y)] + arrived[f, block(y), 1]

        def use_chunk(chunk):
            each_block(chunk * CHUNK, (chunk + 1) * CHUNK, lambda y: use(f, y, *mu(y)))

        def take(chunk):
            def body(y):
                mu_re, mu_im = mu(y)
                co, s = cosine[f, block(y)], sine[f, block(y)]
                re, im = co * mu_re + s * mu_im, co * mu_im - s * mu_re
                put_padded(y, *filter_x(re, im, taps, True))

            each_block(chunk * CHUNK, (chunk + 1) * CHUNK, body)

        def give(chunk):
            def body(y):
                re, im = filter_y(y, taps, True)
                leaving[f, block(y), 0] = re
                leaving[f, block(y), 1] = im

            each_block(chunk * CHUNK, (chunk + 1) * CHUNK, body)
            hop(f, chunk).start()

        for chunk in range(chunks):
            @pl.when(d < depths - 1)
            def _():
                hop(f, chunk).wait_recv()

            before(f, chunk)

            @pl.when(d > 0)
            def _():
                take(chunk)
                if chunk >= lag:
                    give(chunk - lag)
                if chunk == chunks - 1:
                    for last in range(chunks - lag, chunks):
                        give(last)
                use_chunk(chunk)

            @pl.when(d == 0)
            def _():
                use_chunk(chunk)

            taken(f, chunk)

    def push_grad(to, sender):
        return pltpu.make_async_remote_copy(
            src_ref=grad.at[piece(to)], dst_ref=gathered.at[sender],
            send_sem=grad_send.at[to], recv_sem=grad_recv.at[sender],
            device_id={"freq": to}, device_id_type=MESH,
        )

    def send_grad(first, last):
        def step(to, carry):
            @pl.when(to != me)
            def _():
                push_grad(to, me).start()

            return carry

        lax.fori_loop(first, last, step, 0)

    early = d >= depths // 2

    @pl.when(early)
    def _():
        load_adjoint.wait()
        unfold(adjoint_in, adj)
        lax.fori_loop(1, peers, wait_slow, 0)

        def keep(f, y, mu_re, mu_im):
            adj[f, 0, block(y)] = mu_re
            adj[f, 1, block(y)] = mu_im

        @pl.when(d < depths - 1)
        def _():
            each_lane(phases)

        def before(f, chunk):
            @pl.when(d == depths - 1)
            def _():
                phases(f, chunk * CHUNK, (chunk + 1) * CHUNK)

        each_lane(lambda f: chain(f, before, keep, lambda f, chunk: None))
        lax.fori_loop(1, peers, drain_slow, 0)
        load_source.wait()
        unfold(source_in, wave)

        def finish(f, y, re, im):
            re, im = turned(f, y, re, im)
            add_grad(y, adj[f, 1, block(y)] * re - adj[f, 0, block(y)] * im)

        each_lane(lambda f: forward(f, finish))
        send_grad(0, peers)

    @pl.when(jnp.logical_not(early))
    def _():
        load_source.wait()
        unfold(source_in, wave)

        def finish(f, y, re, im):
            wave[f, 0, block(y)] = re
            wave[f, 1, block(y)] = im

        each_lane(lambda f: forward(f, finish))
        load_adjoint.wait()
        unfold(adjoint_in, adj)
        lax.fori_loop(1, peers, wait_slow, 0)

        def turn(f):
            phases(f)

            def body(y):
                re, im = turned(f, y, wave[f, 0, block(y)], wave[f, 1, block(y)])
                wave[f, 0, block(y)] = re
                wave[f, 1, block(y)] = im

            each_block(0, lines, body)

        each_lane(turn)
        lax.fori_loop(1, peers, drain_slow, 0)

        def use(f, y, mu_re, mu_im):
            add_grad(y, mu_im * wave[f, 0, block(y)] - mu_re * wave[f, 1, block(y)])

        def taken(f, chunk):
            @pl.when(f == lanes - 1)
            def _():
                done = [n * CHUNK * peers // lines for n in (chunk, chunk + 1)]
                send_grad(*done)

        each_lane(lambda f: chain(f, lambda f, chunk: None, use, taken))

    gathered[me] = grad[piece(me)]

    def add(i, total):
        push_grad(me, peer(i)).wait_recv()
        return total + gathered[peer(i)]

    total = lax.fori_loop(1, peers, add, gathered[me])
    out_ref[...] = total * (1.0 / count)

    def drain(i, carry):
        push_grad(peer(i), me).wait_send()
        return carry

    lax.fori_loop(1, peers, drain, 0)

    @pl.when(d > 0)
    def _():
        def drain_mu(i, carry):
            hop(i // chunks, i % chunks).wait_send()
            return carry

        lax.fori_loop(0, lanes * chunks, drain_mu, 0)


def on_device(slowness, freq_index, taps, source_top, adjoint_source):
    lanes, _, _, lines, cells = source_top.shape
    peers, depths = lax.axis_size("freq"), lax.axis_size("depth")
    count, _, width = taps.shape
    reach = width // 2
    assert cells == SUB * LANES and slowness.shape[0] == 1
    rows = slowness.shape[1] // LANES
    whole_lines = rows % SUB == 0
    piece = (rows // SUB, SUB, LANES) if whole_lines else (1, rows, LANES)
    pieces = (piece[0] * peers,) + piece[1:]
    line = (SUB, LANES)
    f32 = jnp.float32
    vmem = pl.BlockSpec(memory_space=pltpu.VMEM)
    hbm = pl.BlockSpec(memory_space=pltpu.HBM)
    dma = pltpu.SemaphoreType.DMA
    chunks = lines // CHUNK
    out = pl.pallas_call(
        functools.partial(
            kernel, peers, depths, lanes, lines, reach, count, piece[0], whole_lines
        ),
        out_shape=jax.ShapeDtypeStruct(piece, f32),
        in_specs=[hbm] * 5,
        out_specs=vmem,
        scratch_shapes=[
            pltpu.VMEM(piece, f32),
            pltpu.SMEM((lanes,), jnp.int32),
            pltpu.SMEM((width, 2, count), f32),
            pltpu.VMEM((lanes, 2, lines, cells), f32),
            pltpu.VMEM((lanes, 2, lines, cells), f32),
            pltpu.VMEM((lanes, 2, lines) + line, f32),
            pltpu.VMEM((lanes, 2, lines) + line, f32),
            pltpu.VMEM((3, lines + 2 * reach) + line, f32),
            pltpu.VMEM(pieces, f32),
            pltpu.VMEM((lanes, lines) + line, f32),
            pltpu.VMEM((lanes, lines) + line, f32),
            pltpu.VMEM((lanes, lines, 2) + line, f32),
            pltpu.VMEM((lanes, lines, 2) + line, f32),
            pltpu.VMEM(pieces, f32),
            pltpu.VMEM((peers,) + piece, f32),
            dma((5,)),
            dma((peers,)),
            dma((peers,)),
            dma((lanes * chunks,)),
            dma((lanes * chunks,)),
            dma((peers,)),
            dma((peers,)),
        ],
        compiler_params=pltpu.CompilerParams(
            collective_id=0, has_side_effects=True, vmem_limit_bytes=56 * 1024 * 1024
        ),
    )(
        slowness.reshape(piece),
        freq_index,
        taps.transpose(2, 1, 0),
        source_top.reshape(lanes, 2, lines, cells),
        adjoint_source.reshape(lanes, 2, lines, cells),
    )
    return out.reshape(slowness.shape)


def solution(mesh):
    in_specs = (
        P("depth", "freq"),
        P("freq"),
        P(),
        P("freq", "depth", None, None, None),
        P("freq", "depth", None, None, None),
    )
    out_specs = P("depth", "freq")
    return jax.shard_map(
        on_device, mesh=mesh, in_specs=in_specs, out_specs=out_specs, check_vma=False
    )
```

```python
import functools
import math

import jax
import jax.numpy as jnp
from jax import lax
from jax.experimental import pallas as pl
from jax.experimental.pallas import tpu as pltpu
from jax.sharding import PartitionSpec as P

MESH = pl.DeviceIdType.MESH
LANES = 128
SUB = 8
BLOCK = 4
STEP = 8
CHUNK = 4

PI_HIGH = 3.140625
PI_LOW = math.pi - PI_HIGH


def sin_cos(phase):
    turns = jnp.floor(phase * (1.0 / math.pi) + 0.5)
    rest = (phase - turns * PI_HIGH) - turns * PI_LOW
    sign = 1.0 - 2.0 * (turns - 2.0 * jnp.floor(turns * 0.5))
    square = rest * rest
    odd = -1.0 / math.factorial(11)
    for n, s in ((9, 1), (7, -1), (5, 1), (3, -1), (1, 1)):
        odd = odd * square + s / math.factorial(n)
    even = 1.0 / math.factorial(12)
    for n, s in ((10, -1), (8, 1), (6, -1), (4, 1), (2, -1), (0, 1)):
        even = even * square + s / math.factorial(n)
    return sign * rest * odd, sign * even


def shifter(value):
    lane = lax.broadcasted_iota(jnp.int32, value.shape, 2)
    row = lax.broadcasted_iota(jnp.int32, value.shape, 1)
    after = jnp.where(row < SUB - 1, pltpu.roll(value, SUB - 1, 1), 0.0)
    before = jnp.where(row > 0, pltpu.roll(value, 1, 1), 0.0)

    def shifted(o):
        if o > 0:
            return pltpu.roll(jnp.where(lane >= o, value, after), LANES - o, 2)
        if o < 0:
            return pltpu.roll(jnp.where(lane < LANES + o, value, before), -o, 2)
        return value

    return shifted


def filtered(at, taps, adjoint):
    reach = len(taps) // 2
    total = None
    for k, (t_re, t_im) in enumerate(taps):
        o = reach - k if adjoint else k - reach
        u_re, u_im, u_sum = at(o)
        if adjoint:
            t_im = -t_im
        new = (t_re * u_sum, (t_im - t_re) * u_re, (t_re + t_im) * u_im)
        total = new if total is None else tuple(x + y for x, y in zip(total, new))
    a, b, c = total
    return a - c, a + b


def filter_x(re, im, taps, adjoint):
    shift_re, shift_im = shifter(re), shifter(im)

    def at(o):
        u_re, u_im = shift_re(o), shift_im(o)
        return u_re, u_im, u_re + u_im

    return filtered(at, taps, adjoint)


def kernel(
    peers, depths, lanes, lines, reach, count, per_piece, whole_lines,
    slow_hbm, index_hbm, taps_hbm, source_hbm, adjoint_hbm, out_ref,
    slow_ref, index_ref, taps_ref, source_in, adjoint_in, wave, adj, padded, slow, cosine, sine,
    arrived, leaving, grad, gathered,
    in_sem, slow_send, slow_recv, mu_send, mu_recv, grad_send, grad_recv,
):
    me = lax.axis_index("freq")
    d = lax.axis_index("depth")
    chunks = lines // CHUNK
    per_line = max(1, peers // lines)

    load_slow = pltpu.make_async_copy(slow_hbm, slow_ref, in_sem.at[0])
    load_index = pltpu.make_async_copy(index_hbm, index_ref, in_sem.at[1])
    load_taps = pltpu.make_async_copy(taps_hbm, taps_ref, in_sem.at[2])
    load_adjoint = pltpu.make_async_copy(adjoint_hbm, adjoint_in, in_sem.at[3])
    load_source = pltpu.make_async_copy(source_hbm, source_in, in_sem.at[4])

    barrier = pltpu.get_barrier_semaphore()

    def peer(i):
        return lax.rem(me + i, peers)

    def greet(i, carry):
        pl.semaphore_signal(barrier, inc=1, device_id={"freq": peer(i)}, device_id_type=MESH)
        return carry

    lax.fori_loop(1, peers, greet, 0)

    @pl.when(d < depths - 1)
    def _():
        pl.semaphore_signal(barrier, inc=1, device_id={"depth": d + 1}, device_id_type=MESH)

    for load in (load_slow, load_index, load_taps, load_adjoint, load_source):
        load.start()

    def piece(i):
        return pl.ds(i * per_piece, per_piece)

    margin = jnp.zeros((reach, SUB, LANES), jnp.float32)
    for part in range(3):
        padded[part, pl.ds(0, reach)] = margin
        padded[part, pl.ds(lines + reach, reach)] = margin
    grad[...] = jnp.zeros_like(grad)

    @pl.when(d == depths - 1)
    def _():
        arrived[...] = jnp.zeros_like(arrived)

    load_slow.wait()
    slow[piece(me)] = slow_ref[...]
    pl.semaphore_wait(barrier, jnp.where(d > 0, peers, peers - 1))

    def push_slow(i, sender):
        return pltpu.make_async_remote_copy(
            src_ref=slow_ref, dst_ref=slow.at[piece(sender)],
            send_sem=slow_send.at[peer(i)], recv_sem=slow_recv.at[sender],
            device_id={"freq": peer(i)}, device_id_type=MESH,
        )

    def start_slow(i, carry):
        push_slow(i, me).start()
        return carry

    lax.fori_loop(1, peers, start_slow, 0)
    load_index.wait()
    load_taps.wait()

    def wait_slow(i, carry):
        push_slow(i, peer(i)).wait_recv()
        return carry

    def drain_slow(i, carry):
        push_slow(i, me).wait_send()
        return carry

    def tap_list(f):
        row = index_ref[f]
        return [(taps_ref[k, 0, row], taps_ref[k, 1, row]) for k in range(2 * reach + 1)]

    def angular(f):
        return 8.0 * (index_ref[f].astype(jnp.float32) + 1.0) / count

    def block(y):
        return pl.ds(y, BLOCK)

    def each_block(first, last, body):
        if last - first <= STEP:
            for y in range(first, last, BLOCK):
                body(y)
            return

        def step(b, carry):
            for part in range(STEP // BLOCK):
                body(b * STEP + part * BLOCK)
            return carry

        lax.fori_loop(first // STEP, last // STEP, step, 0)

    def each_lane(body):
        def step(f, carry):
            body(f)
            return carry

        lax.fori_loop(0, lanes, step, 0)

    def unfold(from_ref, to_ref):
        def body(i, carry):
            f, part = i // 2, i % 2
            for t in range(lines // SUB):
                rows = from_ref[f, part, pl.ds(t * SUB, SUB), :]
                to_ref[f, part, pl.ds(t * SUB, SUB)] = rows.reshape(SUB, SUB, LANES)
            return carry

        lax.fori_loop(0, 2 * lanes, body, 0)

    def filter_y(y, taps, adjoint):
        return filtered(
            lambda o: tuple(padded[part, block(y + reach + o)] for part in range(3)),
            taps, adjoint,
        )

    def put_padded(y, re, im):
        padded[0, block(y + reach)] = re
        padded[1, block(y + reach)] = im
        padded[2, block(y + reach)] = re + im

    def slow_block(y):
        if whole_lines:
            return slow[block(y)]
        return slow[pl.ds(y * per_line, BLOCK * per_line)].reshape(BLOCK, SUB, LANES)

    def add_grad(y, term):
        if whole_lines:
            grad[block(y)] += term
        else:
            grad[pl.ds(y * per_line, BLOCK * per_line)] += term.reshape(
                BLOCK * per_line, SUB // per_line, LANES
            )

    def phases(f, first=0, last=lines):
        w = angular(f)

        def body(y):
            s, co = sin_cos(w * slow_block(y))
            sine[f, block(y)] = s
            cosine[f, block(y)] = co

        each_block(first, last, body)

    def forward(f, finish):
        taps = tap_list(f)

        def along_x(y):
            re, im = filter_x(wave[f, 0, block(y)], wave[f, 1, block(y)], taps, False)
            put_padded(y, re, im)

        def along_y(y):
            finish(f, y, *filter_y(y, taps, False))

        each_block(0, lines, along_x)
        each_block(0, lines, along_y)

    def turned(f, y, re, im):
        w, co, s = angular(f), cosine[f, block(y)], sine[f, block(y)]
        return w * (co * re - s * im), w * (s * re + co * im)

    def hop(f, chunk):
        rows = pl.ds(chunk * CHUNK, CHUNK)
        slot = f * chunks + chunk
        return pltpu.make_async_remote_copy(
            src_ref=leaving.at[f, rows], dst_ref=arrived.at[f, rows],
            send_sem=mu_send.at[slot], recv_sem=mu_recv.at[slot],
            device_id={"depth": lax.max(d - 1, 0)}, device_id_type=MESH,
        )

    def chain(f, before, use, taken):
        taps = tap_list(f)
        lag = -(-reach // CHUNK)

        def mu(y):
            return adj[f, 0, block(y)] + arrived[f, block(y), 0], adj[f, 1, block(y)] + arrived[f, block(y), 1]

        def use_chunk(chunk):
            each_block(chunk * CHUNK, (chunk + 1) * CHUNK, lambda y: use(f, y, *mu(y)))

        def take(chunk):
            def body(y):
                mu_re, mu_im = mu(y)
                co, s = cosine[f, block(y)], sine[f, block(y)]
                re, im = co * mu_re + s * mu_im, co * mu_im - s * mu_re
                put_padded(y, *filter_x(re, im, taps, True))

            each_block(chunk * CHUNK, (chunk + 1) * CHUNK, body)

        def give(chunk):
            def body(y):
                re, im = filter_y(y, taps, True)
                leaving[f, block(y), 0] = re
                leaving[f, block(y), 1] = im

            each_block(chunk * CHUNK, (chunk + 1) * CHUNK, body)
            hop(f, chunk).start()

        for chunk in range(chunks):
            @pl.when(d < depths - 1)
            def _():
                hop(f, chunk).wait_recv()

            before(f, chunk)

            @pl.when(d > 0)
            def _():
                take(chunk)
                if chunk >= lag:
                    give(chunk - lag)
                if chunk == chunks - 1:
                    for last in range(chunks - lag, chunks):
                        give(last)
                use_chunk(chunk)

            @pl.when(d == 0)
            def _():
                use_chunk(chunk)

            taken(f, chunk)

    def push_grad(to, sender):
        return pltpu.make_async_remote_copy(
            src_ref=grad.at[piece(to)], dst_ref=gathered.at[sender],
            send_sem=grad_send.at[to], recv_sem=grad_recv.at[sender],
            device_id={"freq": to}, device_id_type=MESH,
        )

    def send_grad(first, last):
        def step(to, carry):
            @pl.when(to != me)
            def _():
                push_grad(to, me).start()

            return carry

        lax.fori_loop(first, last, step, 0)

    early = d >= depths // 2

    @pl.when(early)
    def _():
        load_adjoint.wait()
        unfold(adjoint_in, adj)
        lax.fori_loop(1, peers, wait_slow, 0)

        def keep(f, y, mu_re, mu_im):
            adj[f, 0, block(y)] = mu_re
            adj[f, 1, block(y)] = mu_im

        @pl.when(d < depths - 1)
        def _():
            each_lane(phases)

        def before(f, chunk):
            @pl.when(d == depths - 1)
            def _():
                phases(f, chunk * CHUNK, (chunk + 1) * CHUNK)

        each_lane(lambda f: chain(f, before, keep, lambda f, chunk: None))
        lax.fori_loop(1, peers, drain_slow, 0)
        load_source.wait()
        unfold(source_in, wave)

        def finish(f, y, re, im):
            re, im = turned(f, y, re, im)
            add_grad(y, adj[f, 1, block(y)] * re - adj[f, 0, block(y)] * im)

        each_lane(lambda f: forward(f, finish))
        send_grad(0, peers)

    @pl.when(jnp.logical_not(early))
    def _():
        load_source.wait()
        unfold(source_in, wave)

        def finish(f, y, re, im):
            wave[f, 0, block(y)] = re
            wave[f, 1, block(y)] = im

        each_lane(lambda f: forward(f, finish))
        load_adjoint.wait()
        unfold(adjoint_in, adj)
        lax.fori_loop(1, peers, wait_slow, 0)

        def turn(f):
            phases(f)

            def body(y):
                re, im = turned(f, y, wave[f, 0, block(y)], wave[f, 1, block(y)])
                wave[f, 0, block(y)] = re
                wave[f, 1, block(y)] = im

            each_block(0, lines, body)

        each_lane(turn)
        lax.fori_loop(1, peers, drain_slow, 0)

        def use(f, y, mu_re, mu_im):
            add_grad(y, mu_im * wave[f, 0, block(y)] - mu_re * wave[f, 1, block(y)])

        def taken(f, chunk):
            @pl.when(f == lanes - 1)
            def _():
                done = [n * CHUNK * peers // lines for n in (chunk, chunk + 1)]
                send_grad(*done)

        each_lane(lambda f: chain(f, lambda f, chunk: None, use, taken))

    gathered[me] = grad[piece(me)]

    def add(i, total):
        push_grad(me, peer(i)).wait_recv()
        return total + gathered[peer(i)]

    total = lax.fori_loop(1, peers, add, gathered[me])
    out_ref[...] = total * (1.0 / count)

    def drain(i, carry):
        push_grad(peer(i), me).wait_send()
        return carry

    lax.fori_loop(1, peers, drain, 0)

    @pl.when(d > 0)
    def _():
        def drain_mu(i, carry):
            hop(i // chunks, i % chunks).wait_send()
            return carry

        lax.fori_loop(0, lanes * chunks, drain_mu, 0)


def on_device(slowness, freq_index, taps, source_top, adjoint_source):
    lanes, _, _, lines, cells = source_top.shape
    peers, depths = lax.axis_size("freq"), lax.axis_size("depth")
    count, _, width = taps.shape
    reach = width // 2
    assert cells == SUB * LANES and slowness.shape[0] == 1
    rows = slowness.shape[1] // LANES
    whole_lines = rows % SUB == 0
    piece = (rows // SUB, SUB, LANES) if whole_lines else (1, rows, LANES)
    pieces = (piece[0] * peers,) + piece[1:]
    line = (SUB, LANES)
    f32 = jnp.float32
    vmem = pl.BlockSpec(memory_space=pltpu.VMEM)
    hbm = pl.BlockSpec(memory_space=pltpu.HBM)
    dma = pltpu.SemaphoreType.DMA
    chunks = lines // CHUNK
    out = pl.pallas_call(
        functools.partial(
            kernel, peers, depths, lanes, lines, reach, count, piece[0], whole_lines
        ),
        out_shape=jax.ShapeDtypeStruct(piece, f32),
        in_specs=[hbm] * 5,
        out_specs=vmem,
        scratch_shapes=[
            pltpu.VMEM(piece, f32),
            pltpu.SMEM((lanes,), jnp.int32),
            pltpu.SMEM((width, 2, count), f32),
            pltpu.VMEM((lanes, 2, lines, cells), f32),
            pltpu.VMEM((lanes, 2, lines, cells), f32),
            pltpu.VMEM((lanes, 2, lines) + line, f32),
            pltpu.VMEM((lanes, 2, lines) + line, f32),
            pltpu.VMEM((3, lines + 2 * reach) + line, f32),
            pltpu.VMEM(pieces, f32),
            pltpu.VMEM((lanes, lines) + line, f32),
            pltpu.VMEM((lanes, lines) + line, f32),
            pltpu.VMEM((lanes, lines, 2) + line, f32),
            pltpu.VMEM((lanes, lines, 2) + line, f32),
            pltpu.VMEM(pieces, f32),
            pltpu.VMEM((peers,) + piece, f32),
            dma((5,)),
            dma((peers,)),
            dma((peers,)),
            dma((lanes * chunks,)),
            dma((lanes * chunks,)),
            dma((peers,)),
            dma((peers,)),
        ],
        compiler_params=pltpu.CompilerParams(
            collective_id=0, has_side_effects=True, vmem_limit_bytes=56 * 1024 * 1024
        ),
    )(
        slowness.reshape(piece),
        freq_index,
        taps.transpose(2, 1, 0),
        source_top.reshape(lanes, 2, lines, cells),
        adjoint_source.reshape(lanes, 2, lines, cells),
    )
    return out.reshape(slowness.shape)


def solution(mesh):
    in_specs = (
        P("depth", "freq"),
        P("freq"),
        P(),
        P("freq", "depth", None, None, None),
        P("freq", "depth", None, None, None),
    )
    out_specs = P("depth", "freq")
    return jax.shard_map(
        on_device, mesh=mesh, in_specs=in_specs, out_specs=out_specs, check_vma=False
    )
```
